32 devices in a mesh: section: 2 (over core), fsdp: 2 (over x), ctx: 4 (over z), tp: 2 (over y).
Axes of the slice: x: 2, y: 2, z: 4, core: 2. Of those that a mesh axis runs over, the one named last changes fastest.
Arguments:
- boundary: bfloat16 [2, 2, 2, 1024, 2048], P('section', None, 'fsdp', 'ctx'), may hold values from -6 to 6
- segments: int32 [2, 2, 1024], P(None, 'fsdp'), may hold values from 0 to 2, as said below
- qkv_w: bfloat16 [2, 2048, 8, 384], P('section', ('fsdp', 'ctx'), 'tp'), may hold values from -0.125 to 0.125
- out_w: bfloat16 [2, 2048, 2048], P('section', 'tp', ('fsdp', 'ctx')), may hold values from -2 to 2
- gate_up_w: bfloat16 [2, 2048, 2, 8192], P('section', ('fsdp', 'ctx'), None, 'tp'), may hold values from -0.125 to 0.125
- down_w: bfloat16 [2, 8192, 2048], P('section', 'tp', ('fsdp', 'ctx')), may hold values from -0.0625 to 0.0625
- norm_gains: bfloat16 [2, 2, 2048], P('section', None, ('fsdp', 'ctx')), may hold values from 0.25 to 1.75
Outputs:
- boundary_out: float32 [2, 2, 2, 1024, 2048], P('section', None, 'fsdp', 'ctx')
- grad_qkv_w: float32 [2, 2048, 8, 384], P('section', ('fsdp', 'ctx'), 'tp')
- grad_out_w: float32 [2, 2048, 2048], P('section', 'tp', ('fsdp', 'ctx'))
- grad_gate_up_w: float32 [2, 2048, 2, 8192], P('section', ('fsdp', 'ctx'), None, 'tp')
- grad_down_w: float32 [2, 8192, 2048], P('section', 'tp', ('fsdp', 'ctx'))
- grad_norm_gains: float32 [2, 2048], P('section', ('fsdp', 'ctx'))
- grad_ffn_gains: float32 [2, 2048], P('section', ('fsdp', 'ctx'))
The draws below stay inside these ranges and needn't reach their ends.
Inputs may be any that keep to these rules, and one draw needn't show every extreme that they name: `segments`: each sequence holds three documents numbered 0, 1, 2 in order; each has 204 tokens or more, and document 1 holds positions 511 and 512.
All inputs are finite; a program needn't handle non-finite values.
Results may differ from the reference program's by a relative error of at most 0.03.
Values may be sent and summed in bfloat16 or wider, within the bound.
No kernel may reach another device: no remote copies, remote signals or barrier semaphores. Data moves between devices by JAX's collectives and lax.ppermute only.
A program may use at most 512 MiB of HBM per device.

```python
import jax
import jax.numpy as jnp
from jax import lax

D = 2048
H = 32
KV = 8
HD = 64
FF = 8192
LEN = 1024
MICRO = 2
BATCH = 2
N_TP = 2


def draw_segments(key, part):
    key = jax.random.fold_in(key, 7)
    first_key, second_key = jax.random.split(key)
    cut_one = jax.random.randint(first_key, (MICRO, BATCH, 1), LEN // 5, 3 * LEN // 8 + 1)
    cut_two = jax.random.randint(second_key, (MICRO, BATCH, 1), 5 * LEN // 8, 4 * LEN // 5 + 1)
    places = jnp.arange(LEN, dtype=jnp.int32)[None, None, :]
    return (places >= cut_one).astype(jnp.int32) + (places >= cut_two).astype(jnp.int32)


def shard_levels(own_key, shape, pieces, least, largest):
    level, own = 1.0, jax.random.fold_in(own_key, 6)
    for dim, blocks in pieces:
        heights = jnp.exp(jax.random.uniform(jax.random.fold_in(own, dim), (blocks,), jnp.float32, least / len(pieces), largest / len(pieces)))
        level = level * jnp.repeat(heights, shape[dim] // blocks).reshape([-1 if axis == dim else 1 for axis in range(len(shape))])
    return level


def normal_values(own_key, extent, deviation, reach, shards=(), kind=jnp.bfloat16):
    values = deviation * jax.random.normal(own_key, extent, jnp.float32)
    if shards:
        values = values * shard_levels(own_key, extent, shards, -0.22, 0.18)
    return jnp.clip(values, -reach, reach).astype(kind)


def setup_inputs(seed: int = 0) -> dict:
    key_list = jax.random.split(jax.random.key(seed), 8)
    return {
        "boundary": normal_values(key_list[0], (2, MICRO, BATCH, LEN, D), 1.0, 6.0, ((0, 2), (2, 2), (3, 4))),
        "segments": draw_segments(jax.random.fold_in(key_list[7], 71), 0),
        "qkv_w": normal_values(key_list[2], (2, D, KV, (H // KV + 2) * HD), D ** -0.5, 0.125, ((0, 2), (1, 8), (2, 2))),
        "out_w": normal_values(key_list[3], (2, H * HD, D), (max(1, H * HD * 4 // LEN)) ** -0.5, 2.0, ((0, 2), (1, 2), (2, 8))),
        "gate_up_w": normal_values(key_list[4], (2, D, 2, FF), D ** -0.5, 0.125, ((0, 2), (1, 8), (3, 2))),
        "down_w": normal_values(key_list[5], (2, FF, D), FF ** -0.5, 0.0625, ((0, 2), (1, 2), (2, 8))),
        "norm_gains": jnp.clip(1.0 + 0.15 * jax.random.normal(key_list[6], (2, 2, D), jnp.float32), 0.25, 1.75).astype(jnp.bfloat16),
    }


@jax.custom_vjp
def low(v):
    return lax.optimization_barrier(v.astype(jnp.bfloat16)).astype(jnp.float32)

@jax.custom_vjp
def low_back(v):
    return v

def low_keep(v):
    return (low(v), None)

def low_pass(kept, grad):
    return (grad,)

def back_keep(v):
    return (v, None)

def back_low(kept, grad):
    return (low(grad),)
low.defvjp(low_keep, low_pass)
low_back.defvjp(back_keep, back_low)
norm_eps = 1e-05
rope_base = 500000.0
masked_score = -1e+30
highest = lax.Precision.HIGHEST

def rotate(values, cosine, sine):
    half_dim = values.shape[-1] // 2
    turned = jnp.concatenate([-values[..., half_dim:], values[..., :half_dim]], axis=-1)
    return values * cosine + turned * sine

def rope_tables(positions):
    freq_index = jnp.arange(HD // 2, dtype=jnp.float32)
    inverse = rope_base ** (-2.0 * freq_index / HD)
    angles = positions.astype(jnp.float32)[:, None] * inverse[None, :]
    angles = jnp.concatenate([angles, angles], axis=-1)
    return (jnp.cos(angles), jnp.sin(angles))

def normalize(values, gain):
    return values * lax.rsqrt(lax.optimization_barrier(jnp.mean(values * values, axis=-1, keepdims=True)) + norm_eps) * gain

def layer(params, inputs, seg_row):
    qkv_weight, out_weight, gate_up_weight, down_weight, gains = params
    groups = H // KV
    scale = HD ** (-0.5)
    offsets = jnp.arange(LEN, dtype=jnp.int32)
    starts = lax.optimization_barrier(jnp.sum((seg_row[None, :] < seg_row[:, None]).astype(jnp.int32), axis=1))
    cosine, sine = rope_tables(offsets - starts)
    attn_in = low(normalize(inputs, gains[0]))
    qkv = low_back(jnp.einsum('ld,dkc->lkc', attn_in, qkv_weight, precision=highest))
    queries = low(rotate(qkv[:, :, :groups * HD].reshape(LEN, KV, groups, HD), cosine[:, None, None, :], sine[:, None, None, :]))
    keys = low(rotate(qkv[:, :, groups * HD:(groups + 1) * HD], cosine[:, None, :], sine[:, None, :]))
    values = low(qkv[:, :, (groups + 1) * HD:])
    block_rows = min(512, LEN)
    block_count = LEN // block_rows

    def attend(item):
        query_block, block_index = item
        first_row = block_index * block_rows
        query_pos = first_row + jnp.arange(block_rows, dtype=jnp.int32)
        query_seg = lax.dynamic_slice_in_dim(seg_row, first_row, block_rows)
        scores = low_back(jnp.einsum('qkgd,tkd->kgqt', query_block, keys, precision=highest) * scale)
        allowed = (offsets[None, :] <= query_pos[:, None]) & (seg_row[None, :] == query_seg[:, None])
        scores = jnp.where(allowed[None, None], scores, masked_score)
        top_score = lax.optimization_barrier(jnp.max(scores, axis=-1, keepdims=True))
        weights = jnp.exp(scores - top_score)
        probs = low(weights / lax.optimization_barrier(jnp.sum(weights, axis=-1, keepdims=True)))
        return jnp.einsum('kgqt,tkd->qkgd', probs, values, precision=highest)
    attended = lax.map(jax.checkpoint(attend), (queries.reshape(block_count, block_rows, KV, groups, HD), jnp.arange(block_count, dtype=jnp.int32)))
    attended = low(low_back(attended.reshape(LEN, H * HD)))
    head_part = jnp.einsum('lgk,gkd->lgd', attended.reshape(LEN, N_TP, H * HD // N_TP), out_weight.reshape(N_TP, H * HD // N_TP, D), precision=highest)
    middle = inputs + low_back(lax.optimization_barrier(jnp.sum(low(head_part), axis=1)))
    ffn_in = low(normalize(middle, gains[1]))
    gate_up = low_back(jnp.einsum('ld,dtf->ltf', ffn_in, gate_up_weight, precision=highest))
    hidden = low(jax.nn.silu(gate_up[:, 0]) * gate_up[:, 1])
    unit_part = jnp.einsum('lgf,gfd->lgd', hidden.reshape(LEN, N_TP, FF // N_TP), down_weight.reshape(N_TP, FF // N_TP, D), precision=highest)
    return middle + low_back(lax.optimization_barrier(jnp.sum(low(unit_part), axis=1)))

def reference(boundary, segments, qkv_w, out_w, gate_up_w, down_w, norm_gains):
    seq_count = MICRO * BATCH
    block_in = boundary[0].astype(jnp.float32).reshape(seq_count, LEN, D)
    cotangent = boundary[1].astype(jnp.float32).reshape(seq_count, LEN, D)
    seg_rows = segments.reshape(seq_count, LEN)
    params = tuple((weight.astype(jnp.float32) for weight in (qkv_w, out_w, gate_up_w, down_w, norm_gains)))

    def network(weights, sequences):

        def one_sequence(carry, item):
            sequence, seg_row = item
            first_params = tuple((weight[0] for weight in weights))
            second_params = tuple((weight[1] for weight in weights))
            section_zero = layer(first_params, sequence, seg_row)
            return (carry, layer(second_params, low(section_zero), seg_row))
        carry_out, results = lax.scan(jax.checkpoint(one_sequence), jnp.zeros((), jnp.float32), (sequences, seg_rows))
        return results
    results, pullback = jax.vjp(network, params, block_in)
    grad_params, grad_in = pullback(cotangent)
    boundary_out = jnp.stack([grad_in, results]).reshape(2, MICRO, BATCH, LEN, D)
    return (boundary_out, grad_params[0], grad_params[1], grad_params[2], grad_params[3], grad_params[4][:, 0], grad_params[4][:, 1])
```

```python
from functools import partial

import jax
import jax.numpy as jnp
from jax import lax
from jax.experimental import pallas as pl
from jax.experimental.pallas import tpu as pltpu
from jax.sharding import PartitionSpec as P

H = 32
KV = 8
HD = 64
GROUPS = H // KV

norm_eps = 1e-05
rope_base = 500000.0
masked_score = -1e30

f32 = jnp.float32
bf16 = jnp.bfloat16


def from_behind(value, axis, by):
    size = lax.axis_size(axis)
    pairs = [(i, i + by) for i in range(size) if 0 <= i + by < size]
    return lax.ppermute(value, axis, pairs)


def rotate(values, cosine, sine):
    half_dim = values.shape[-1] // 2
    turned = jnp.concatenate([-values[..., half_dim:], values[..., :half_dim]], axis=-1)
    return values * cosine + turned * sine


def rope_tables(positions):
    freq_index = jnp.arange(HD // 2, dtype=jnp.float32)
    inverse = rope_base ** (-2.0 * freq_index / HD)
    angles = positions.astype(jnp.float32)[:, None] * inverse[None, :]
    angles = jnp.concatenate([angles, angles], axis=-1)
    return (jnp.cos(angles), jnp.sin(angles))


def context_info(seg_full, ctx_index, rows):
    offsets = jnp.arange(rows, dtype=jnp.int32)
    query_pos = ctx_index * rows + offsets
    query_seg = lax.dynamic_slice_in_dim(seg_full, ctx_index * rows, rows)
    starts = jnp.sum((seg_full[None, :] < query_seg[:, None]).astype(jnp.int32), axis=1)
    cosine, sine = rope_tables(query_pos - starts)
    key_pos = jnp.arange(seg_full.shape[0], dtype=jnp.int32)
    return (cosine, sine, query_pos, query_seg, key_pos, seg_full)


def norm_rows(values, gain):
    scale_rows = lax.rsqrt(jnp.mean(values * values, axis=-1, keepdims=True) + norm_eps)
    return (values * scale_rows * gain, scale_rows)


def plain_norm_back(values, scale_rows, gain, grad_normed):
    scaled = values * scale_rows
    grad_gain = jnp.sum(grad_normed * scaled, axis=0)
    grad_hat = grad_normed * gain
    grad_in = scale_rows * (grad_hat - scaled * jnp.mean(grad_hat * scaled, axis=-1, keepdims=True))
    return (grad_in, grad_gain)


def block_scores(query_block, pair, info):
    cosine, sine, query_pos, query_seg, key_pos, key_seg = info
    raw = jnp.einsum(
        "qkgd,tkd->kgqt", query_block, pair[0], preferred_element_type=jnp.float32
    ) * HD ** (-0.5)
    allowed = (key_pos[None, :] <= query_pos[:, None]) & (key_seg[None, :] == query_seg[:, None])
    return jnp.where(allowed[None, None], raw, masked_score)


def plain_attend_forward(queries, pair, info):
    rows, kv_local, groups, head_dim = queries.shape
    block_rows = min(512, rows)
    block_count = rows // block_rows

    def one_block(item):
        query_block, block_index = item
        scores = block_scores(query_block, pair, info)
        top_score = jnp.max(scores, axis=-1, keepdims=True)
        weights = jnp.exp(scores - top_score)
        totals = jnp.sum(weights, axis=-1, keepdims=True)
        probs = (weights / totals).astype(jnp.bfloat16)
        output = jnp.einsum("kgqt,tkd->qkgd", probs, pair[1], preferred_element_type=jnp.float32)
        return (output, (top_score + jnp.log(totals))[..., 0])

    blocks = queries.reshape(block_count, block_rows, kv_local, groups, head_dim)
    outputs, log_sums = lax.map(one_block, (blocks, jnp.arange(block_count, dtype=jnp.int32)))
    return (outputs.reshape(rows, kv_local, groups, head_dim), log_sums)


def plain_attend_backward(queries, pair, log_sums, grad_attended, info):
    rows, kv_local, groups, head_dim = queries.shape
    block_rows = min(512, rows)
    block_count = rows // block_rows
    scale = HD ** (-0.5)

    def step_block(carry, item):
        grad_keys, grad_values = carry
        query_block, grad_block, lse_block, block_index = item
        scores = block_scores(query_block, pair, info)
        probs = jnp.exp(scores - lse_block[..., None])
        grad_probs = jnp.einsum(
            "qkgd,tkd->kgqt", grad_block, pair[1], preferred_element_type=jnp.float32
        )
        delta = jnp.sum(probs * grad_probs, axis=-1, keepdims=True)
        grad_scores = (probs * (grad_probs - delta)).astype(jnp.bfloat16)
        grad_query = (
            jnp.einsum("kgqt,tkd->qkgd", grad_scores, pair[0], preferred_element_type=jnp.float32)
            * scale
        )
        grad_keys = (
            grad_keys
            + jnp.einsum(
                "kgqt,qkgd->tkd", grad_scores, query_block, preferred_element_type=jnp.float32
            )
            * scale
        )
        grad_values = grad_values + jnp.einsum(
            "kgqt,qkgd->tkd",
            probs.astype(jnp.bfloat16),
            grad_block,
            preferred_element_type=jnp.float32,
        )
        return ((grad_keys, grad_values), grad_query)

    start_grads = jnp.zeros(pair.shape[1:], jnp.float32)
    blocks = queries.reshape(block_count, block_rows, kv_local, groups, head_dim)
    grad_blocks = grad_attended.reshape(block_count, block_rows, kv_local, groups, head_dim)
    carry_out, grad_queries = lax.scan(
        step_block,
        (start_grads, start_grads),
        (blocks, grad_blocks, log_sums, jnp.arange(block_count, dtype=jnp.int32)),
    )
    return (
        grad_queries.reshape(rows, kv_local, groups, head_dim),
        jnp.stack([carry_out[0], carry_out[1]]),
    )


def feed_forward_in(middle, scale_two, gains, gate_up_full):
    ffn_in = (middle * scale_two * gains[1]).astype(jnp.bfloat16)
    gate_up = jnp.einsum("rd,dtf->rtf", ffn_in, gate_up_full, preferred_element_type=jnp.float32)
    hidden_low = (jax.nn.silu(gate_up[:, 0]) * gate_up[:, 1]).astype(jnp.bfloat16)
    return (ffn_in, gate_up, hidden_low)


def layer_forward(inputs, weights, info):
    qkv_full, out_full, gate_up_full, down_full, gains = weights
    cosine, sine = (info[0], info[1])
    rows = inputs.shape[0]
    full_rows = info[5].shape[0]
    kv_local = qkv_full.shape[1]
    groups = H // KV
    normed_one, scale_one = norm_rows(inputs, gains[0])
    attn_in = normed_one.astype(jnp.bfloat16)
    qkv = jnp.einsum("rd,dkc->rkc", attn_in, qkv_full, preferred_element_type=jnp.float32)
    queries = rotate(
        qkv[:, :, : groups * HD].reshape(rows, kv_local, groups, HD),
        cosine[:, None, None, :],
        sine[:, None, None, :],
    ).astype(jnp.bfloat16)
    keys_now = rotate(
        qkv[:, :, groups * HD : (groups + 1) * HD], cosine[:, None, :], sine[:, None, :]
    ).astype(jnp.bfloat16)
    values_now = qkv[:, :, (groups + 1) * HD :].astype(jnp.bfloat16)
    own_pair = jnp.stack([keys_now, values_now]).reshape(2, rows, kv_local * HD)
    pair = lax.all_gather(own_pair, "ctx", axis=1, tiled=True).reshape(2, full_rows, kv_local, HD)
    attended, log_sums = plain_attend_forward(queries, pair, info)
    attended_low = attended.reshape(rows, kv_local * groups * HD).astype(jnp.bfloat16)
    middle = inputs + lax.psum(
        jnp.dot(attended_low, out_full, preferred_element_type=jnp.float32).astype(jnp.bfloat16),
        "tp",
    ).astype(jnp.float32)
    normed_two, scale_two = norm_rows(middle, gains[1])
    ffn_in, gate_up, hidden_low = feed_forward_in(middle, scale_two, gains, gate_up_full)
    result = middle + lax.psum(
        jnp.dot(hidden_low, down_full, preferred_element_type=jnp.float32).astype(jnp.bfloat16),
        "tp",
    ).astype(jnp.float32)
    ff_saved = (ffn_in, gate_up, hidden_low)
    return (
        result,
        (
            inputs,
            scale_one,
            attn_in,
            queries,
            pair,
            log_sums,
            attended_low,
            middle,
            scale_two,
            ff_saved,
        ),
    )


def layer_backward(saved, grad_out, weights, info):
    qkv_full, out_full, gate_up_full, down_full, gains = weights
    (
        inputs,
        scale_one,
        attn_in,
        queries,
        pair,
        log_sums,
        attended_low,
        middle,
        scale_two,
        ff_saved,
    ) = saved
    cosine, sine = (info[0], info[1])
    rows, kv_local, groups, head_dim = queries.shape
    full_rows = pair.shape[1]
    ffn_in, gate_up, hidden_low = ff_saved
    grad_low = grad_out.astype(jnp.bfloat16)
    grad_down = jnp.einsum("rf,rd->fd", hidden_low, grad_low, preferred_element_type=jnp.float32)
    grad_hidden = jnp.einsum("rd,fd->rf", grad_low, down_full, preferred_element_type=jnp.float32)
    gate = gate_up[:, 0]
    sigma = jax.nn.sigmoid(gate)
    grad_gate = grad_hidden * gate_up[:, 1] * sigma * (1.0 + gate * (1.0 - sigma))
    grad_up = grad_hidden * gate * sigma
    grad_pair_ff = jnp.stack([grad_gate, grad_up], axis=1).astype(jnp.bfloat16)
    grad_gate_up = jnp.einsum(
        "rd,rtf->dtf", ffn_in, grad_pair_ff, preferred_element_type=jnp.float32
    )
    grad_ffn_in = lax.psum(
        jnp.einsum(
            "rtf,dtf->rd", grad_pair_ff, gate_up_full, preferred_element_type=jnp.float32
        ).astype(jnp.bfloat16),
        "tp",
    ).astype(jnp.float32)
    grad_mid_norm, grad_gain_two = plain_norm_back(middle, scale_two, gains[1], grad_ffn_in)
    grad_middle = grad_out + grad_mid_norm
    grad_attn_low = grad_middle.astype(jnp.bfloat16)
    grad_out_proj = jnp.einsum(
        "rh,rd->hd", attended_low, grad_attn_low, preferred_element_type=jnp.float32
    )
    grad_attended = jnp.einsum(
        "rd,hd->rh", grad_attn_low, out_full, preferred_element_type=jnp.float32
    ).astype(jnp.bfloat16)
    grad_queries, grad_pair = plain_attend_backward(
        queries, pair, log_sums, grad_attended.reshape(rows, kv_local, groups, head_dim), info
    )
    returned = lax.psum_scatter(
        grad_pair.reshape(2, full_rows, kv_local * head_dim).astype(jnp.bfloat16),
        "ctx",
        scatter_dimension=1,
        tiled=True,
    ).astype(jnp.float32)
    own_grad = returned.reshape(2, rows, kv_local, head_dim)
    grad_q_raw = rotate(grad_queries, cosine[:, None, None, :], -sine[:, None, None, :]).reshape(
        rows, kv_local, groups * head_dim
    )
    grad_k_raw = rotate(own_grad[0], cosine[:, None, :], -sine[:, None, :])
    grad_qkv = jnp.concatenate([grad_q_raw, grad_k_raw, own_grad[1]], axis=-1).astype(jnp.bfloat16)
    grad_qkv_proj = jnp.einsum("rd,rkc->dkc", attn_in, grad_qkv, preferred_element_type=jnp.float32)
    grad_attn_in = lax.psum(
        jnp.einsum("rkc,dkc->rd", grad_qkv, qkv_full, preferred_element_type=jnp.float32).astype(
            jnp.bfloat16
        ),
        "tp",
    ).astype(jnp.float32)
    grad_in_norm, grad_gain_one = plain_norm_back(inputs, scale_one, gains[0], grad_attn_in)
    grads = (
        grad_qkv_proj,
        grad_out_proj,
        grad_gate_up,
        grad_down,
        jnp.stack([grad_gain_one, grad_gain_two]),
    )
    return (grad_middle + grad_in_norm, grads)


def pick_section(is_first, first_value, second_value):
    return jnp.where(is_first, first_value, second_value)


def scale_by(factor, values):
    return values * factor


def local(boundary, segments, qkv_w, out_w, gate_up_w, down_w, norm_gains):
    micro_count = boundary.shape[1]
    rows = boundary.shape[3]
    width = boundary.shape[4]
    is_first = lax.axis_index("section") == 0
    ctx_index = lax.axis_index("ctx")
    local_ends = boundary[0, :, 0]
    seg_all = segments[:, 0]
    gathered = (
        lax.all_gather(qkv_w[0], ("fsdp", "ctx"), axis=0, tiled=True),
        lax.all_gather(out_w[0], ("fsdp", "ctx"), axis=1, tiled=True),
        lax.all_gather(gate_up_w[0], ("fsdp", "ctx"), axis=0, tiled=True),
        lax.all_gather(down_w[0], ("fsdp", "ctx"), axis=1, tiled=True),
        lax.all_gather(norm_gains[0], ("fsdp", "ctx"), axis=1, tiled=True),
    )
    weights = (gathered[0], gathered[1], gathered[2], gathered[3], gathered[4].astype(jnp.float32))
    chooser = partial(pick_section, is_first)
    received = jnp.zeros((rows, width), jnp.bfloat16)
    saved_list = []
    info_list = []
    outputs_list = []
    for tick_index in range(micro_count + 1):
        own_index = min(tick_index, micro_count - 1)
        prior_index = max(tick_index - 1, 0)
        seg_full = jnp.where(is_first, seg_all[own_index], seg_all[prior_index])
        info = context_info(seg_full, ctx_index, rows)
        inputs = jnp.where(is_first, local_ends[own_index], received).astype(jnp.float32)
        result, saved = layer_forward(inputs, weights, info)
        saved_list.append(saved)
        info_list.append(info)
        outputs_list.append(result)
        if tick_index < micro_count:
            received = from_behind(result.astype(jnp.bfloat16), "section", 1)
    grad_received = jnp.zeros((rows, width), jnp.float32)
    totals = None
    grad_list = []
    for tick_index in range(micro_count + 1):
        early = max(tick_index - 1, 0)
        late = min(tick_index + 1, micro_count)
        saved = jax.tree.map(chooser, saved_list[early], saved_list[late])
        info = jax.tree.map(chooser, info_list[early], info_list[late])
        own_grad = local_ends[min(tick_index, micro_count - 1)].astype(jnp.float32)
        grad_out = jnp.where(is_first, grad_received, own_grad)
        grad_inputs, grads = layer_backward(saved, grad_out, weights, info)
        valid = jnp.where(is_first, tick_index >= 1, tick_index < micro_count).astype(jnp.float32)
        grads = jax.tree.map(partial(scale_by, valid), grads)
        totals = grads if totals is None else jax.tree.map(jnp.add, totals, grads)
        grad_list.append(grad_inputs)
        if tick_index < micro_count:
            grad_received = from_behind(grad_inputs.astype(jnp.bfloat16), "section", -1).astype(
                grad_inputs.dtype
            )
    totals = (
        lax.psum_scatter(
            totals[0].astype(jnp.bfloat16), ("fsdp", "ctx"), scatter_dimension=0, tiled=True
        ).astype(jnp.float32),
        lax.psum_scatter(
            totals[1].astype(jnp.bfloat16), ("fsdp", "ctx"), scatter_dimension=1, tiled=True
        ).astype(jnp.float32),
        lax.psum_scatter(
            totals[2].astype(jnp.bfloat16), ("fsdp", "ctx"), scatter_dimension=0, tiled=True
        ).astype(jnp.float32),
        lax.psum_scatter(
            totals[3].astype(jnp.bfloat16), ("fsdp", "ctx"), scatter_dimension=1, tiled=True
        ).astype(jnp.float32),
        lax.psum_scatter(
            totals[4].astype(jnp.bfloat16), ("fsdp", "ctx"), scatter_dimension=1, tiled=True
        ).astype(jnp.float32),
    )
    ends_out = jnp.stack(
        [
            jnp.where(is_first, grad_list[micro_index + 1], outputs_list[micro_index + 1])
            for micro_index in range(micro_count)
        ]
    )
    return (
        ends_out[None, :, None],
        totals[0][None],
        totals[1][None],
        totals[2][None],
        totals[3][None],
        totals[4][0][None],
        totals[4][1][None],
    )


def swap_core(value):
    return lax.ppermute(value, "section", [(0, 1), (1, 0)])


def swap_tp(value):
    return lax.ppermute(value, "tp", [(0, 1), (1, 0)])


def swap_fsdp(value):
    return lax.ppermute(value, "fsdp", [(0, 1), (1, 0)])


def swap_ctx(value, m):
    return lax.ppermute(value, "ctx", [(i ^ m, i) for i in range(lax.axis_size("ctx"))])


def pick(bit, first, second):
    return jnp.where(bit == 0, first, second)


def ring(value):
    size = lax.axis_size("ctx")
    return lax.ppermute(value, "ctx", [(i, (i + 1) % size) for i in range(size)])


def ring_back(value):
    size = lax.axis_size("ctx")
    return lax.ppermute(value, "ctx", [((i + 1) % size, i) for i in range(size)])


class Flow:
    def __init__(self):
        self.values, self.next, self.last, self.first = {}, {}, None, None

    def put(self, name, n, value):
        self.values[name, n] = value

    def get(self, name, n):
        return self.values[name, n]

    def send(self, name, n, move, value, made=False):
        if self.last is not None:
            if made:
                self.next[self.last] = value
                self.first = value if self.first is None else self.first
            value, _ = lax.optimization_barrier((value, self.values[self.last]))
        self.put(name, n, move(value))
        self.last = (name, n)

    def point(self, name, n, value):
        names = DUE.get((name, n), ())
        if names or isinstance(value, tuple):
            ready = [self.next[k] for k in names if k in self.next]
            value, *got = lax.optimization_barrier((value, *[self.values[k] for k in names], *ready))
            self.values.update(zip(names, got))
        return value


def dot(a, b, dims):
    return lax.dot_general(a, b, (dims, ((), ())), preferred_element_type=f32)


NN = ((1,), (0,))
NT = ((1,), (1,))
TN = ((0,), (0,))
VMEM = pl.BlockSpec(memory_space=pltpu.VMEM)
SMEM = pl.BlockSpec(memory_space=pltpu.SMEM)
COST_SCALE = 0.1
VMEM_MIB = 28
A_MID, A_IN, ATT, S_MID, S_HALF, MIDDLE, B_MID, B_IN, HIDDEN, R_MID, R_HALF, RESULT = range(12)
G_MID, G_IN, D_HID, C_MID, C_HALF, D_MID, M_MID, M_IN, D_OUT, D_KEYS, D_QKV, E_MID, E_HALF, D_IN = range(12, 26)
A0, F0, F1, F2, F3, E0, E1, E2, E3, H1, H2, H3, HX, ATTN_SUM = range(14)
G1, G2, G3, GX, FFN_SUM, L1, L2, L3, LX, LOW_SUM, ENDS = range(17, 28)
DUE = {
    (HIDDEN, 0): ((ENDS, 1),),
    (RESULT, 0): ((F1, 1),),
    (S_MID, 1): ((F2, 1),),
    (C_MID, 1): ((G1, 1),),
    (M_MID, 1): ((L1, 1),),
    (D_OUT, 1): ((G2, 1),),
    (D_QKV, 1): ((L2, 1),),
    (D_IN, 1): ((G3, 1),),
    (D_HID, 0): ((L3, 1), (GX, 1)),
    (D_MID, 0): ((H3, 1), (LX, 1)),
    (D_OUT, 0): ((G1, 0),),
    (D_KEYS, 0): ((L1, 0), (HX, 1)),
    (D_IN, 0): ((H3, 0),),
}


def call(kernel, outs, ins, flops, name, **kw):
    args = dict(in_specs=[SMEM if v.dtype == jnp.int32 and v.ndim == 1 else VMEM for v in ins], out_specs=[VMEM] * len(outs))
    args.update(kw)
    return pl.pallas_call(
        kernel,
        out_shape=[jax.ShapeDtypeStruct(s, d) for s, d in outs],
        cost_estimate=pl.CostEstimate(flops=int(flops * COST_SCALE), bytes_accessed=1024, transcendentals=0),
        compiler_params=pltpu.CompilerParams(vmem_limit_bytes=VMEM_MIB * 2**20),
        name=name.__name__,
        **args,
    )(*ins)


def views(refs):
    return [r if k is None else r.at[k] for r in refs for k in ([None] if len(r.shape) == 2 else range(r.shape[0]))]


def block_spec(array, width, where):
    if array.ndim == 2:
        return pl.BlockSpec((array.shape[0], width), lambda t: (0, where(t)))
    return pl.BlockSpec(array.shape[:2] + (width,), lambda t: (0, 0, where(t)))


def cols(index, width):
    return pl.ds(pl.multiple_of(index * width, width), width)


def rope(x, cosine, sin_up, sin_down):
    return x * cosine + pltpu.roll(x, 96, 1) * sin_up + pltpu.roll(x, 32, 1) * sin_down


def kv_tables(cosine, sin_up, sin_down):
    is_key = lax.broadcasted_iota(jnp.int32, cosine.shape, 1) < HD
    return (jnp.where(is_key, cosine, 1.0), jnp.where(is_key, sin_up, 0.0), jnp.where(is_key, sin_down, 0.0))


def qkv_forward(order, spots, near, far, tables, blocks):
    rows, width = near.shape
    nb = order.shape[0]
    bw = width // nb
    qw = GROUPS * HD
    part_rows = rows // 4

    def kernel(order, spots, near, far, cosine, sin_up, sin_down, *refs):
        w, (q_ref, kv_ref, wide) = views(refs[:-3]), refs[-3:]
        for k in range(nb):
            wide[cols(order[k], bw), :] = w[k][:, : qw + 2 * HD]
        for part, a in enumerate((near, far)):
            for half in range(2):
                acc = dot(a[half * 2 * part_rows : (half + 1) * 2 * part_rows, :], wide[...], NN)
                for t in range(2):
                    there = cols(spots[4 * part + 2 * half + t], part_rows)
                    v = acc[t * part_rows : (t + 1) * part_rows, :]
                    tabs = (cosine[there, :], sin_up[there, :], sin_down[there, :])
                    for j in range(qw // 128):
                        here = slice(128 * j, 128 * (j + 1))
                        q_ref[there, here] = (rope(v[:, here], *tabs) * HD**-0.5).astype(bf16)
                    kv_ref[there, :] = rope(v[:, qw:], *kv_tables(*tabs)).astype(bf16)

    return call(
        kernel,
        [((2 * rows, qw), bf16), ((2 * rows, 2 * HD), bf16)],
        [order, spots, near, far, *tables, *blocks],
        2 * 2 * rows * width * (qw + 2 * HD),
        qkv_forward,
        scratch_shapes=[pltpu.VMEM((width, qw + 2 * HD), bf16)],
    )


def keep_mask(start, first, rows, keys):
    q_pos = first + lax.broadcasted_iota(jnp.int32, (rows, keys), 0)
    k_pos = lax.broadcasted_iota(jnp.int32, (rows, keys), 1)
    return jnp.where((k_pos <= q_pos) & (k_pos >= start), 0.0, masked_score)


def attend_forward(spots, q, kv, start):
    total, qw = q.shape
    rows = total // 4
    part_rows = total // 8

    def kernel(spots, q_ref, kv_ref, start_ref, att_ref, lse_ref):
        for i in range(4):
            here = slice(i * rows, (i + 1) * rows)
            keys = (i + 1) * rows
            k, v = kv_ref[:keys, :HD], kv_ref[:keys, HD:]
            bias = keep_mask(start_ref[here, :], i * rows, rows, keys)
            for g in range(GROUPS):
                head = slice(g * HD, (g + 1) * HD)
                s = dot(q_ref[here, head], k, NT) + bias
                top = jnp.max(s, axis=1, keepdims=True)
                p = jnp.exp(s - top)
                norm = jnp.sum(p, axis=1, keepdims=True)
                o = (dot(p.astype(bf16), v, NN) / norm).astype(bf16)
                for t in range(2):
                    att_ref[cols(spots[2 * i + t], part_rows), head] = o[t * part_rows : (t + 1) * part_rows, :]
                lse_ref[here, g : g + 1] = top + jnp.log(norm)

    return call(
        kernel,
        [((total, qw), bf16), ((total, GROUPS), f32)],
        [spots, q, kv, start],
        2 * 2 * total * total * qw,
        attend_forward,
    )


def attend_backward(spots, q, kv, lse, grad, start, tables):
    total, qw = q.shape
    rows = total // 4
    part_rows = total // 8

    def kernel(spots, q_ref, kv_ref, lse_ref, g_ref, start_ref, cosine, sin_up, sin_down, out, dq, dkv):
        dkv[...] = jnp.zeros_like(dkv)
        for i in range(4):
            here = slice(i * rows, (i + 1) * rows)
            keys = (i + 1) * rows
            k, v = kv_ref[:keys, :HD], kv_ref[:keys, HD:]
            bias = keep_mask(start_ref[here, :], i * rows, rows, keys)
            grads = jnp.concatenate([g_ref[cols(spots[2 * i + t], part_rows), :] for t in range(2)], axis=0)
            for g in range(GROUPS):
                head = slice(g * HD, (g + 1) * HD)
                qh, gh = q_ref[here, head], grads[:, head]
                p = jnp.exp(dot(qh, k, NT) + bias - lse_ref[here, g : g + 1])
                dp = dot(gh, v, NT)
                delta = jnp.sum(p * dp, axis=1, keepdims=True)
                ds = (p * (dp - delta)).astype(bf16)
                dq[here, head] = dot(ds, k, NN) * HD**-0.5
                dkv[:keys, :HD] += dot(ds, qh, TN)
                dkv[:keys, HD:] += dot(p.astype(bf16), gh, TN)
        for j in range(8):
            here, there = slice(j * part_rows, (j + 1) * part_rows), cols(spots[j], part_rows)
            tabs = (cosine[here, :], -sin_up[here, :], -sin_down[here, :])
            for b in range(qw // 128):
                out[there, 128 * b : 128 * (b + 1)] = rope(dq[here, 128 * b : 128 * (b + 1)], *tabs).astype(bf16)
            out[there, qw:] = rope(dkv[here, :], *kv_tables(*tabs)).astype(bf16)

    return call(
        kernel,
        [((total, qw + 2 * HD), bf16)],
        [spots, q, kv, lse, grad, start, *tables],
        5 * 2 * total * total * qw,
        attend_backward,
        scratch_shapes=[pltpu.VMEM((total, qw), f32), pltpu.VMEM((total, 2 * HD), f32)],
    )[0]


def project_out(order, values, blocks, first_col, out_type, part):
    total, depth = values.shape
    rows = total // 2
    nb = order.shape[0]
    bw = blocks[0].shape[-2]
    whole = first_col % depth != 0

    def kernel(order, v_ref, *refs):
        w, out = views(refs[:-1]), refs[-1]
        base = first_col if whole else 0
        for k in range(nb):
            acc = dot(v_ref[:, :bw], w[k][:, base : base + bw], NN)
            for j in range(1, depth // bw):
                acc += dot(v_ref[:, j * bw : (j + 1) * bw], w[k][:, base + j * bw : base + (j + 1) * bw], NN)
            out[:, cols(order[k], bw)] = acc.astype(out.dtype)

    return call(
        kernel,
        [((rows, nb * bw), out_type)],
        [order, values, *blocks],
        2 * rows * depth * nb * bw,
        project_out,
        grid=(1,),
        in_specs=[SMEM, pl.BlockSpec((rows, depth), lambda t: (part, 0))]
        + [block_spec(b, b.shape[-1] if whole else depth, lambda t: 0 if whole else first_col // depth) for b in blocks],
        out_specs=[pl.BlockSpec((rows, nb * bw), lambda t: (0, 0))],
    )[0]


def ffn_forward(order, near, far, blocks, units):
    rows, width = near.shape
    nb = order.shape[0]
    bw = width // nb
    tile = min(256, units)
    tiles = units // tile

    def kernel(order, near, far, *refs):
        hid, by_gate, by_up, wide = refs[-4:]
        w = views(refs[:-4])
        for k in range(nb):
            wide[0, cols(order[k], bw), :] = w[k][...]
            wide[1, cols(order[k], bw), :] = w[nb + k][...]
        for part, a in enumerate((near, far)):
            here = slice(part * rows, (part + 1) * rows)
            gate = dot(a[...], wide[0], NN)
            up = dot(a[...], wide[1], NN)
            sigma = 1.0 / (1.0 + jnp.exp(-gate))
            silu = gate * sigma
            hid[here, :] = (silu * up).astype(bf16)
            by_gate[here, :] = (up * sigma * (1.0 + gate * (1.0 - sigma))).astype(bf16)
            by_up[here, :] = silu.astype(bf16)

    all_rows = pl.BlockSpec((rows, width), lambda t: (0, 0))
    return call(
        kernel,
        [((2 * rows, units), bf16)] * 3,
        [order, near, far, *blocks, *blocks],
        2 * 2 * rows * width * 2 * units,
        ffn_forward,
        grid=(tiles,),
        in_specs=[SMEM, all_rows, all_rows]
        + [block_spec(b, tile, lambda t: t) for b in blocks]
        + [block_spec(b, tile, lambda t: t + tiles) for b in blocks],
        out_specs=[pl.BlockSpec((2 * rows, tile), lambda t: (0, t))] * 3,
        scratch_shapes=[pltpu.VMEM((2, width, tile), bf16)],
    )


def ffn_backward(order, near, far, by_gate, by_up, blocks):
    rows, width = near.shape
    nb = order.shape[0]
    units = by_gate.shape[1]
    bw = width // nb

    def kernel(order, near, far, by_gate, by_up, *refs):
        d_gate, d_up, wide = refs[-3:]
        w = views(refs[:-3])
        for k in range(nb):
            wide[:, cols(order[k], bw)] = w[k][...]
        for part, a in enumerate((near, far)):
            here = slice(part * rows, (part + 1) * rows)
            acc = dot(a[...], wide[...], NT)
            d_gate[here, :] = (acc * by_gate[here, :].astype(f32)).astype(bf16)
            d_up[here, :] = (acc * by_up[here, :].astype(f32)).astype(bf16)

    all_rows = pl.BlockSpec((rows, width), lambda t: (0, 0))
    tall = pl.BlockSpec((2 * rows, bw), lambda t: (0, t))
    return call(
        kernel,
        [((2 * rows, units), bf16)] * 2,
        [order, near, far, by_gate, by_up, *blocks],
        2 * 2 * rows * width * units,
        ffn_backward,
        grid=(units // bw,),
        in_specs=[SMEM, all_rows, all_rows, tall, tall]
        + [block_spec(b, bw, lambda t: 2 * units // bw + t) for b in blocks],
        out_specs=[tall] * 2,
        scratch_shapes=[pltpu.VMEM((bw, width), bf16)],
    )


def ffn_input_grad(order, d_gate, d_up, blocks):
    total, units = d_gate.shape
    rows = total // 2
    nb = order.shape[0]
    bw = blocks[0].shape[-2]

    def kernel(order, dg, du, *refs):
        far, near, slots, sems = refs[-4:]
        w = views(refs[:-4])

        def fetch(k):
            return pltpu.make_async_copy(w[k].at[:, : 2 * units], slots.at[k % 2], sems.at[k % 2])

        fetch(0).start()
        for k in range(nb):
            if k + 1 < nb:
                fetch(k + 1).start()
            fetch(k).wait()
            here = cols(order[k], bw)
            for out, part in ((near, 0), (far, 1)):
                tokens = slice(part * rows, (part + 1) * rows)
                acc = dot(dg[tokens, :], slots[k % 2, :, :units], NT) + dot(du[tokens, :], slots[k % 2, :, units:], NT)
                out[:, here] = acc.astype(out.dtype)

    return call(
        kernel,
        [((rows, nb * bw), bf16), ((rows, nb * bw), f32)],
        [order, d_gate, d_up, *blocks],
        2 * total * 2 * units * nb * bw,
        ffn_input_grad,
        in_specs=[SMEM, VMEM, VMEM] + [pl.BlockSpec(memory_space=pl.ANY)] * len(blocks),
        scratch_shapes=[pltpu.VMEM((2, bw, 2 * units), bf16), pltpu.SemaphoreType.DMA((2,))],
    )


def block_columns(rows, width, places):
    return [pl.BlockSpec((rows, width), lambda t, order, p=p: (0, order[p])) for p in places for _ in range(4)]


def turn(left, first, turned):
    rows, width = left[0].shape
    for p in range(len(left) // 4):
        for part in range(2):
            turned[p * width : (p + 1) * width, part * rows : (part + 1) * rows] = left[4 * p + first + part][...].T


def store(out, acc, got, here=slice(None)):
    width = out.shape[1]
    for p in range(out.shape[0]):
        value = acc[p * width : (p + 1) * width]
        for r in got:
            value += r[p, :, here].astype(f32)
        out[p, :, here] = value.astype(bf16)


def ffn_grad(order, near, far, d_gate, d_up, hidden, grad_near, grad_far, side, m, *received):
    total, units = d_gate.shape
    rows, width = near.shape
    bw = width // order.shape[0]
    tile = min(512, units // 2)
    tiles = units // tile
    steps = tiles if side else 2 * tiles
    begin = 2 * tiles * side

    def kernel(order, dg, du, h, *refs):
        left, got, out, turned = refs[:8], refs[8:-2], refs[-2], refs[-1]
        step = pl.program_id(0)
        t = step + begin
        pl.when((step == 0) & (t < 2 * tiles))(lambda: turn(left, 0, turned))
        pl.when(t == 2 * tiles)(lambda: turn(left, 2, turned))
        pl.when(t < tiles)(lambda: store(out, dot(turned[...], dg[...], NN), got))
        pl.when((t >= tiles) & (t < 2 * tiles))(lambda: store(out, dot(turned[...], du[...], NN), got))
        pl.when(t >= 2 * tiles)(lambda: store(out, dot(turned[...], h[...], NN), got))

    def tall(first):
        return pl.BlockSpec((total, tile), lambda t, order: (0, jnp.clip(t + begin - first * tiles, 0, tiles - 1)))

    part = pl.BlockSpec((2, bw, tile), lambda t, order: (0, 0, t))
    return pl.pallas_call(
        kernel,
        out_shape=jax.ShapeDtypeStruct((2, bw, steps * tile), bf16),
        grid_spec=pltpu.PrefetchScalarGridSpec(
            num_scalar_prefetch=1,
            grid=(steps,),
            in_specs=[tall(0), tall(1), tall(2)] + block_columns(rows, bw, (2 * m, 2 * m + 1)) + [part] * len(received),
            out_specs=part,
            scratch_shapes=[pltpu.VMEM((2 * bw, total), bf16)],
        ),
        cost_estimate=pl.CostEstimate(flops=int(4 * total * steps * tile * bw * COST_SCALE), bytes_accessed=1024, transcendentals=0),
        compiler_params=pltpu.CompilerParams(vmem_limit_bytes=VMEM_MIB * 2**20),
        name=ffn_grad.__name__,
    )(order, d_gate, d_up, hidden, *([near, far, grad_near, grad_far] * 2), *received)


def attn_grad(order, near, far, d_qkv, attended, grad_near, grad_far, m, *received):
    total, nq = d_qkv.shape
    rows, width = near.shape
    bw = width // order.shape[0]

    def kernel(order, dq, att, *refs):
        left, got, out = refs[:8], refs[8:-1], refs[-1]
        for p in range(2):
            near, far, gn, gf = left[4 * p : 4 * p + 4]
            value = dot(near[...], dq[:rows, :], TN) + dot(far[...], dq[rows:, :], TN)
            for r in got:
                value += r[p, :, :nq].astype(f32)
            out[p, :, :nq] = value.astype(bf16)
            value = dot(att[:rows, :], gn[...], TN) + dot(att[rows:, :], gf[...], TN)
            for r in got:
                value += r[p, :, nq:].astype(f32)
            out[p, :, nq:] = value.astype(bf16)

    def whole(shape):
        return pl.BlockSpec(shape, lambda t, order: (0,) * len(shape))

    shape = (2, bw, nq + bw)
    return pl.pallas_call(
        kernel,
        out_shape=jax.ShapeDtypeStruct(shape, bf16),
        grid_spec=pltpu.PrefetchScalarGridSpec(
            num_scalar_prefetch=1,
            grid=(1,),
            in_specs=[whole(d_qkv.shape), whole(attended.shape)]
            + block_columns(rows, bw, (2 * m, 2 * m + 1))
            + [whole(shape)] * len(received),
            out_specs=whole(shape),
        ),
        cost_estimate=pl.CostEstimate(flops=int(4 * total * (nq + bw) * bw * COST_SCALE), bytes_accessed=1024, transcendentals=0),
        compiler_params=pltpu.CompilerParams(vmem_limit_bytes=VMEM_MIB * 2**20),
        name=attn_grad.__name__,
    )(order, d_qkv, attended, *([near, far, grad_near, grad_far] * 2), *received)


def out_backward(order, near, far, blocks):
    rows, width = near.shape
    nb = order.shape[0]
    bw = width // nb
    qw = GROUPS * HD

    def kernel(order, near, far, *refs):
        w, out = views(refs[:-1]), refs[-1]
        for part, a in enumerate((near, far)):
            acc = dot(a[:, cols(order[0], bw)], w[0][:, qw + 2 * HD :], NT)
            for k in range(1, nb):
                acc += dot(a[:, cols(order[k], bw)], w[k][:, qw + 2 * HD :], NT)
            out[part * rows : (part + 1) * rows, :] = acc.astype(bf16)

    return call(
        kernel, [((2 * rows, qw), bf16)], [order, near, far, *blocks], 2 * 2 * rows * width * qw, out_backward
    )[0]


def qkv_backward(order, d_qkv, blocks):
    total, nq = d_qkv.shape
    rows = total // 2
    nb = order.shape[0]
    bw = blocks[0].shape[-2]

    def kernel(order, d_ref, *refs):
        w, (far_out, near_out) = views(refs[:-2]), refs[-2:]
        for k in range(nb):
            here = cols(order[k], bw)
            far_out[:, here] = dot(d_ref[rows:, :], w[k][:, :nq], NT).astype(bf16)
            near_out[:, here] = dot(d_ref[:rows, :], w[k][:, :nq], NT)

    return call(
        kernel,
        [((rows, nb * bw), bf16), ((rows, nb * bw), f32)],
        [order, d_qkv, *blocks],
        2 * total * nb * bw * nq,
        qkv_backward,
    )


def gather_group(flow, point, n, block):
    half = block.shape[0] // 2
    beside, pair, far_block = flow.point(point, n, (swap_tp(block), swap_fsdp(block), swap_core(block)))
    last = jnp.concatenate((swap_tp(pair[:half]), swap_fsdp(beside[half:])), axis=0)
    far_pair, far_beside = swap_core(pair), swap_core(beside)
    last, far_pair, far_beside = flow.point(point + 1, n, (last, far_pair, far_beside))
    near = jnp.concatenate((block, beside, pair, last), axis=0)
    return (near, jnp.concatenate((far_block, far_beside, far_pair, swap_core(last)), axis=0))


def sum_group(flow, point, n, near, far):
    half = far.shape[0] // 2
    high = flow.point(point, n, near[half:] + swap_core(far[half:]).astype(f32))
    low = near[:half] + swap_core(far[:half]).astype(f32)
    half //= 2
    split = half // 2
    last = high[half:].astype(bf16)
    by_tp, by_fsdp = flow.point(point + 1, n, (swap_tp(last[:split]), swap_fsdp(last[split:])))
    pair = jnp.concatenate((high[:split] + by_tp.astype(f32), high[split:half]), axis=0).astype(bf16)
    beside = jnp.concatenate((low[half : half + split], low[half + split :] + by_fsdp.astype(f32)), axis=0).astype(bf16)
    return low[:half] + swap_tp(beside).astype(f32) + swap_fsdp(pair).astype(f32)


def row_scale(values):
    return lax.rsqrt(jnp.mean(values * values, axis=-1, keepdims=True) + norm_eps)


def group_layer(flow, n, state, attn_w, gains, order, spots, start, tables):
    scale_one = row_scale(state)
    a_near, a_far = gather_group(flow, A_MID, n, (state * scale_one * gains[0]).astype(bf16))
    q, kv = qkv_forward(order, spots, a_near, a_far, tables, attn_w)
    attended, lse = attend_forward(spots, q, kv, start)
    attended = flow.point(ATT, n, attended)
    first_col = kv.shape[1] + q.shape[1]
    far = project_out(order, attended, attn_w, first_col, bf16, 1)
    near = project_out(order, attended, attn_w, first_col, f32, 0)
    middle = flow.point(MIDDLE, n, state + sum_group(flow, S_MID, n, near, far))
    scale_two = row_scale(middle)
    b_near, b_far = gather_group(flow, B_MID, n, (middle * scale_two * gains[1]).astype(bf16))
    ffn_w = [flow.get(k, n) for k in ((F0, F1, F2, F3) if n else (F0, E0, F1, E1, F2, E2, F3, E3))]
    units = ffn_w[0].shape[-1] // 3
    hidden, by_gate, by_up = ffn_forward(order, b_near, b_far, ffn_w, units)
    hidden = flow.point(HIDDEN, n, hidden)
    far = project_out(order, hidden, ffn_w, 2 * units, bf16, 1)
    near = project_out(order, hidden, ffn_w, 2 * units, f32, 0)
    result = flow.point(RESULT, n, middle + sum_group(flow, R_MID, n, near, far))
    kept = (attn_w, ffn_w, state, scale_one, a_near, a_far, q, kv, attended, lse)
    return (result, kept + (middle, scale_two, b_near, b_far, hidden, by_gate, by_up))


def norm_back(values, scale_rows, gain, grad_normed):
    scaled = values * scale_rows
    grad_gain = jnp.sum(grad_normed * scaled, axis=0)
    grad_hat = grad_normed * gain
    grad_in = scale_rows * (grad_hat - scaled * jnp.mean(grad_hat * scaled, axis=-1, keepdims=True))
    return (grad_in, grad_gain)


def send_back(flow, n, makes, names):
    last = [make(3) for make in makes]
    for m in (2, 1, 0):
        for k, make in enumerate(makes):
            flow.send(names[k][2 - m], n, ring_back, last[k], True)
        last = [make(m, flow.get(names[k][2 - m], n)) for k, make in enumerate(makes)]
        if m:
            yield last[0]
    for k in range(len(makes)):
        flow.put(names[k][3], n, swap_fsdp(last[k][1]))
        flow.put(names[k][4], n, last[k][0])
    yield last[0]


def group_layer_back(flow, n, saved, grad_out, gains, order, spots, start, tables):
    (attn_w, ffn_w, state, scale_one, a_near, a_far, q, kv, attended, lse) = saved[:10]
    (middle, scale_two, b_near, b_far, hidden, by_gate, by_up) = saved[10:]
    g_near, g_far = gather_group(flow, G_MID, n, grad_out.astype(bf16))
    d_gate, d_up = ffn_backward(order, g_near, g_far, by_gate, by_up, ffn_w)
    d_gate = flow.point(D_HID, n, d_gate)
    makes = [partial(ffn_grad, order, b_near, b_far, d_gate, d_up, hidden, g_near, g_far, side) for side in range(2)]
    rounds = send_back(flow, n, makes, ((G1, G2, G3, GX, FFN_SUM), (L1, L2, L3, LX, LOW_SUM)))
    next(rounds)
    if n:
        next(rounds), next(rounds)
        d_gate, _ = lax.optimization_barrier((d_gate, flow.first))
    far, near = ffn_input_grad(order, d_gate, d_up, ffn_w)
    grad_mid, gain_two = norm_back(middle, scale_two, gains[1], sum_group(flow, C_MID, n, near, far))
    grad_mid = flow.point(D_MID, n, grad_mid + grad_out)
    m_near, m_far = gather_group(flow, M_MID, n, grad_mid.astype(bf16))
    d_att = flow.point(D_OUT, n, out_backward(order, m_near, m_far, attn_w))
    d_qkv = flow.point(D_KEYS, n, attend_backward(spots, q, kv, lse, d_att, start, tables))
    far, near = qkv_backward(order, d_qkv, attn_w)
    make_attn = partial(attn_grad, order, a_near, a_far, d_qkv, attended, m_near, m_far)
    for _ in send_back(flow, n, [make_attn], ((H1, H2, H3, HX, ATTN_SUM),)):
        pass
    for _ in rounds:
        pass
    far = flow.point(D_QKV, n, far)
    grad_in, gain_one = norm_back(state, scale_one, gains[0], sum_group(flow, E_MID, n, near, far))
    return (flow.point(D_IN, n, grad_mid + grad_in), (gain_one, gain_two))


def local_group(boundary, segments, qkv_w, out_w, gate_up_w, down_w, norm_gains):
    nz = lax.axis_size("ctx")
    s, x, z, y = (lax.axis_index(a) for a in ("section", "fsdp", "ctx", "tp"))
    rows, width = boundary.shape[3:]
    own_rows = rows // 2

    ends = lax.dynamic_slice_in_dim(boundary[0, :, 0], y * own_rows, own_rows, axis=1)

    def moves(micro, core):
        return [
            ((core * 2 + f) * nz + c, (c // 2 * 2 + c % 2) * nz + 2 * micro + f) for f in range(2) for c in range(nz)
        ]

    axes = ("section", "fsdp", "ctx")
    late = lax.div(z, 2)
    came = [lax.ppermute(ends[t], axes, moves(t, 0)) for t in range(2)]
    state = pick(late, came[0], came[1]).astype(f32)

    g = norm_gains[0].astype(f32)
    other = swap_core(g)
    g = jnp.concatenate([pick(s, g, other), pick(s, other, g)], axis=0)
    bit = 1
    while bit < nz:
        other = swap_ctx(g, bit)
        side = lax.rem(lax.div(z, bit), 2)
        g = jnp.concatenate([pick(side, g, other), pick(side, other, g)], axis=1)
        bit *= 2
    other = swap_fsdp(g)
    gains = jnp.concatenate([pick(x, g, other), pick(x, other, g)], axis=1).reshape(2, 2, width)

    def parts_of(cut):
        mine, pair = cut(x, s), cut(1 - x, s)
        got = swap_core(jnp.stack([cut(x, 1 - s), cut(1 - x, 1 - s)]))
        return [(pick(s ^ k, mine, got[0]), pick(s ^ k, pair, got[1])) for k in range(2)]

    heads = qkv_w.shape[3]
    head_rows = out_w.shape[1] // 4
    units = gate_up_w.shape[3] // 4
    block = qkv_w.shape[1]
    qkv_own = qkv_w[0].reshape(block, -1)

    def cut_attn(p, c):
        k = 2 * p + c
        left = lax.dynamic_slice_in_dim(qkv_own, k * heads, heads, axis=1)
        right = lax.dynamic_slice_in_dim(out_w[0], k * head_rows, head_rows, axis=0)
        return jnp.concatenate([left, right], axis=1)

    def cut_ffn(p, c):
        k = 2 * p + c
        gate_up = lax.dynamic_slice_in_dim(gate_up_w[0], k * units, units, axis=2)
        down = lax.dynamic_slice_in_dim(down_w[0], k * units, units, axis=0)
        panels = [down[j * block : (j + 1) * block] for j in range(units // block)]
        return jnp.concatenate([gate_up[:, 0], gate_up[:, 1]] + panels, axis=1)

    flow = Flow()

    attn_parts = parts_of(cut_attn)
    pairs = swap_fsdp(jnp.stack([attn_parts[n][1] for n in range(2)]))
    line = [jnp.stack([attn_parts[0][0], pairs[0], attn_parts[1][0], pairs[1]])]
    line[0], state = lax.optimization_barrier((line[0], state))
    gate_up_w, down_w, first, gains = lax.optimization_barrier((gate_up_w, down_w, line[0], gains))
    line = [first]
    for m in range(3):
        flow.send(A0, m, ring, line[-1])
        line.append(flow.get(A0, m))
    attn_w = [[v[2 * n : 2 * n + 2] for v in line] for n in range(2)]
    ffn_parts = parts_of(cut_ffn)
    flow.put(F0, 0, ffn_parts[0][0])
    flow.put(E0, 0, swap_fsdp(ffn_parts[0][1]))
    for m in range(3):
        flow.send((F1, F2, F3)[m], 0, ring, flow.get((F0, F1, F2)[m], 0))
        flow.send((E1, E2, E3)[m], 0, ring, flow.get((E0, E1, E2)[m], 0))
    flow.put(F0, 1, jnp.stack([ffn_parts[1][0], swap_fsdp(ffn_parts[1][1])]))
    for m in range(3):
        flow.send((F1, F2, F3)[m], 1, ring, flow.get((F0, F1, F2)[m], 1))
    ends, _ = lax.optimization_barrier((ends, flow.get(E3, 0)))
    came = [lax.ppermute(ends[t], axes, moves(t, 1)) for t in range(2)]
    flow.put(ENDS, 1, pick(late, came[0], came[1]))

    order = jnp.stack([(x ^ i) * nz + lax.rem(z + nz - m, nz) for m in range(nz) for i in range(2)]).astype(jnp.int32)

    spots = jnp.stack([(4 * s + 2 * x + y) ^ k for k in range(8)]).astype(jnp.int32)
    batch = lax.rem(z, 2)
    seg_here = segments[:, 0].astype(f32)
    seg_all = pick(batch ^ x, seg_here, swap_fsdp(seg_here))
    seg = pick(late, seg_all[0], seg_all[1])
    start = jnp.sum((seg[None, :] < seg[:, None]).astype(jnp.int32), axis=1)
    pos = jnp.arange(seg.shape[0], dtype=jnp.int32)
    lane = jnp.arange(128)
    inverse = rope_base ** (-2.0 * (lane % (HD // 2)).astype(f32) / HD)
    angles = (pos - start).astype(f32)[:, None] * inverse[None, :]
    cosine, sine = jnp.cos(angles), jnp.sin(angles)
    low_half = (lane % HD) < HD // 2
    tables = (cosine, jnp.where(low_half, -sine, 0.0), jnp.where(low_half, 0.0, sine))

    start = start[:, None]
    state, kept_0 = group_layer(flow, 0, state, attn_w[0], gains[0], order, spots, start, tables)
    state = state.astype(bf16).astype(f32)
    final, kept_1 = group_layer(flow, 1, state, attn_w[1], gains[1], order, spots, start, tables)

    grad, gains_1 = group_layer_back(flow, 1, kept_1, flow.get(ENDS, 1).astype(f32), gains[1], order, spots, start, tables)
    grad, gains_0 = group_layer_back(flow, 0, kept_0, grad, gains[0], order, spots, start, tables)
    grads = [
        [(flow.get(own, n), flow.get(pair, n)) for own, pair in ((ATTN_SUM, HX), (FFN_SUM, GX), (LOW_SUM, LX))]
        for n in range(2)
    ]
    gain_grads = [gains_0, gains_1]

    grad, final, _ = lax.optimization_barrier((grad, final, flow.get(L3, 0)))
    went = [
        [lax.ppermute(v.astype(bf16), axes, [(b, a) for a, b in moves(t, core)]) for t in range(2)]
        for core, v in enumerate((grad, final))
    ]
    both = jnp.stack([pick(s, went[0][t], went[1][t]) for t in range(2)])
    other = swap_tp(both)
    ends_out = jnp.concatenate([pick(y, both, other), pick(y, other, both)], axis=1).astype(f32)

    def settle(which):
        (mine_0, pair_0), (mine_1, pair_1) = grads[0][which], grads[1][which]
        mine, pair = pick(s, mine_0, mine_1), pick(s, pair_0, pair_1)
        got = swap_core(jnp.stack([pick(s, mine_1, mine_0), pick(s, pair_1, pair_0)]))
        first = (pick(x, mine, pair), pick(x, got[0], got[1]))
        second = (pick(x, pair, mine), pick(x, got[1], got[0]))
        return [pick(s ^ c, *half) for half in (first, second) for c in range(2)]

    attn = settle(0)
    grad_qkv = jnp.stack([v[:, :heads] for v in attn], axis=1).astype(f32)
    grad_out = jnp.concatenate([v[:, heads:] for v in attn], axis=0).astype(f32)
    ffn = settle(1)
    grad_gate_up = jnp.stack(
        [jnp.concatenate([v[:, t * units : (t + 1) * units] for v in ffn], axis=1) for t in range(2)], axis=1
    ).astype(f32)
    grad_down = jnp.concatenate(settle(2), axis=1).T.astype(f32)

    g = [jnp.stack(pair) for pair in gain_grads]
    g = pick(s, g[0], g[1]) + swap_core(pick(s, g[1], g[0]))

    def fold(value, side, swap):
        half = value.shape[1] // 2
        first, second = value[:, :half], value[:, half:]
        return pick(side, first, second) + swap(pick(side, second, first))

    g = fold(g, x, swap_fsdp)
    g = g + swap_tp(g)
    g, _ = lax.optimization_barrier((g, flow.get(L3, 0)))
    bit = nz // 2
    while bit:
        g = fold(g, lax.rem(lax.div(z, bit), 2), lambda v: swap_ctx(v, bit))
        bit //= 2

    return (ends_out[None, :, None], grad_qkv[None], grad_out[None], grad_gate_up[None], grad_down[None], g[0][None], g[1][None])


def solution(mesh):
    size = mesh.shape
    grouped = size["section"] == size["fsdp"] == size["tp"] == 2 and size["ctx"] == 4 and KV // size["tp"] == 4
    return jax.shard_map(
        local_group if grouped else local,
        mesh=mesh,
        in_specs=(
            P("section", None, "fsdp", "ctx", None),
            P(None, "fsdp", None),
            P("section", ("fsdp", "ctx"), "tp", None),
            P("section", "tp", ("fsdp", "ctx")),
            P("section", ("fsdp", "ctx"), None, "tp"),
            P("section", "tp", ("fsdp", "ctx")),
            P("section", None, ("fsdp", "ctx")),
        ),
        out_specs=(
            P("section", None, "fsdp", "ctx", None),
            P("section", ("fsdp", "ctx"), "tp", None),
            P("section", "tp", ("fsdp", "ctx")),
            P("section", ("fsdp", "ctx"), None, "tp"),
            P("section", "tp", ("fsdp", "ctx")),
            P("section", ("fsdp", "ctx")),
            P("section", ("fsdp", "ctx")),
        ),
        check_vma=False,
    )
```

```python
from functools import partial

import jax
import jax.numpy as jnp
from jax import lax
from jax.experimental import pallas as pl
from jax.experimental.pallas import tpu as pltpu
from jax.sharding import PartitionSpec as P

H = 32
KV = 8
HD = 64
GROUPS = H // KV

norm_eps = 1e-05
rope_base = 500000.0
masked_score = -1e30

f32 = jnp.float32
bf16 = jnp.bfloat16


def from_behind(value, axis, by):
    size = lax.axis_size(axis)
    pairs = [(i, i + by) for i in range(size) if 0 <= i + by < size]
    return lax.ppermute(value, axis, pairs)


def rotate(values, cosine, sine):
    half_dim = values.shape[-1] // 2
    turned = jnp.concatenate([-values[..., half_dim:], values[..., :half_dim]], axis=-1)
    return values * cosine + turned * sine


def rope_tables(positions):
    freq_index = jnp.arange(HD // 2, dtype=jnp.float32)
    inverse = rope_base ** (-2.0 * freq_index / HD)
    angles = positions.astype(jnp.float32)[:, None] * inverse[None, :]
    angles = jnp.concatenate([angles, angles], axis=-1)
    return (jnp.cos(angles), jnp.sin(angles))


def context_info(seg_full, ctx_index, rows):
    offsets = jnp.arange(rows, dtype=jnp.int32)
    query_pos = ctx_index * rows + offsets
    query_seg = lax.dynamic_slice_in_dim(seg_full, ctx_index * rows, rows)
    starts = jnp.sum((seg_full[None, :] < query_seg[:, None]).astype(jnp.int32), axis=1)
    cosine, sine = rope_tables(query_pos - starts)
    key_pos = jnp.arange(seg_full.shape[0], dtype=jnp.int32)
    return (cosine, sine, query_pos, query_seg, key_pos, seg_full)


def norm_rows(values, gain):
    scale_rows = lax.rsqrt(jnp.mean(values * values, axis=-1, keepdims=True) + norm_eps)
    return (values * scale_rows * gain, scale_rows)


def plain_norm_back(values, scale_rows, gain, grad_normed):
    scaled = values * scale_rows
    grad_gain = jnp.sum(grad_normed * scaled, axis=0)
    grad_hat = grad_normed * gain
    grad_in = scale_rows * (grad_hat - scaled * jnp.mean(grad_hat * scaled, axis=-1, keepdims=True))
    return (grad_in, grad_gain)


def block_scores(query_block, pair, info):
    cosine, sine, query_pos, query_seg, key_pos, key_seg = info
    raw = jnp.einsum(
        "qkgd,tkd->kgqt", query_block, pair[0], preferred_element_type=jnp.float32
    ) * HD ** (-0.5)
    allowed = (key_pos[None, :] <= query_pos[:, None]) & (key_seg[None, :] == query_seg[:, None])
    return jnp.where(allowed[None, None], raw, masked_score)


def plain_attend_forward(queries, pair, info):
    rows, kv_local, groups, head_dim = queries.shape
    block_rows = min(512, rows)
    block_count = rows // block_rows

    def one_block(item):
        query_block, block_index = item
        scores = block_scores(query_block, pair, info)
        top_score = jnp.max(scores, axis=-1, keepdims=True)
        weights = jnp.exp(scores - top_score)
        totals = jnp.sum(weights, axis=-1, keepdims=True)
        probs = (weights / totals).astype(jnp.bfloat16)
        output = jnp.einsum("kgqt,tkd->qkgd", probs, pair[1], preferred_element_type=jnp.float32)
        return (output, (top_score + jnp.log(totals))[..., 0])

    blocks = queries.reshape(block_count, block_rows, kv_local, groups, head_dim)
    outputs, log_sums = lax.map(one_block, (blocks, jnp.arange(block_count, dtype=jnp.int32)))
    return (outputs.reshape(rows, kv_local, groups, head_dim), log_sums)


def plain_attend_backward(queries, pair, log_sums, grad_attended, info):
    rows, kv_local, groups, head_dim = queries.shape
    block_rows = min(512, rows)
    block_count = rows // block_rows
    scale = HD ** (-0.5)

    def step_block(carry, item):
        grad_keys, grad_values = carry
        query_block, grad_block, lse_block, block_index = item
        scores = block_scores(query_block, pair, info)
        probs = jnp.exp(scores - lse_block[..., None])
        grad_probs = jnp.einsum(
            "qkgd,tkd->kgqt", grad_block, pair[1], preferred_element_type=jnp.float32
        )
        delta = jnp.sum(probs * grad_probs, axis=-1, keepdims=True)
        grad_scores = (probs * (grad_probs - delta)).astype(jnp.bfloat16)
        grad_query = (
            jnp.einsum("kgqt,tkd->qkgd", grad_scores, pair[0], preferred_element_type=jnp.float32)
            * scale
        )
        grad_keys = (
            grad_keys
            + jnp.einsum(
                "kgqt,qkgd->tkd", grad_scores, query_block, preferred_element_type=jnp.float32
            )
            * scale
        )
        grad_values = grad_values + jnp.einsum(
            "kgqt,qkgd->tkd",
            probs.astype(jnp.bfloat16),
            grad_block,
            preferred_element_type=jnp.float32,
        )
        return ((grad_keys, grad_values), grad_query)

    start_grads = jnp.zeros(pair.shape[1:], jnp.float32)
    blocks = queries.reshape(block_count, block_rows, kv_local, groups, head_dim)
    grad_blocks = grad_attended.reshape(block_count, block_rows, kv_local, groups, head_dim)
    carry_out, grad_queries = lax.scan(
        step_block,
        (start_grads, start_grads),
        (blocks, grad_blocks, log_sums, jnp.arange(block_count, dtype=jnp.int32)),
    )
    return (
        grad_queries.reshape(rows, kv_local, groups, head_dim),
        jnp.stack([carry_out[0], carry_out[1]]),
    )


def feed_forward_in(middle, scale_two, gains, gate_up_full):
    ffn_in = (middle * scale_two * gains[1]).astype(jnp.bfloat16)
    gate_up = jnp.einsum("rd,dtf->rtf", ffn_in, gate_up_full, preferred_element_type=jnp.float32)
    hidden_low = (jax.nn.silu(gate_up[:, 0]) * gate_up[:, 1]).astype(jnp.bfloat16)
    return (ffn_in, gate_up, hidden_low)


def layer_forward(inputs, weights, info):
    qkv_full, out_full, gate_up_full, down_full, gains = weights
    cosine, sine = (info[0], info[1])
    rows = inputs.shape[0]
    full_rows = info[5].shape[0]
    kv_local = qkv_full.shape[1]
    groups = H // KV
    normed_one, scale_one = norm_rows(inputs, gains[0])
    attn_in = normed_one.astype(jnp.bfloat16)
    qkv = jnp.einsum("rd,dkc->rkc", attn_in, qkv_full, preferred_element_type=jnp.float32)
    queries = rotate(
        qkv[:, :, : groups * HD].reshape(rows, kv_local, groups, HD),
        cosine[:, None, None, :],
        sine[:, None, None, :],
    ).astype(jnp.bfloat16)
    keys_now = rotate(
        qkv[:, :, groups * HD : (groups + 1) * HD], cosine[:, None, :], sine[:, None, :]
    ).astype(jnp.bfloat16)
    values_now = qkv[:, :, (groups + 1) * HD :].astype(jnp.bfloat16)
    own_pair = jnp.stack([keys_now, values_now]).reshape(2, rows, kv_local * HD)
    pair = lax.all_gather(own_pair, "ctx", axis=1, tiled=True).reshape(2, full_rows, kv_local, HD)
    attended, log_sums = plain_attend_forward(queries, pair, info)
    attended_low = attended.reshape(rows, kv_local * groups * HD).astype(jnp.bfloat16)
    middle = inputs + lax.psum(
        jnp.dot(attended_low, out_full, preferred_element_type=jnp.float32).astype(jnp.bfloat16),
        "tp",
    ).astype(jnp.float32)
    normed_two, scale_two = norm_rows(middle, gains[1])
    ffn_in, gate_up, hidden_low = feed_forward_in(middle, scale_two, gains, gate_up_full)
    result = middle + lax.psum(
        jnp.dot(hidden_low, down_full, preferred_element_type=jnp.float32).astype(jnp.bfloat16),
        "tp",
    ).astype(jnp.float32)
    ff_saved = (ffn_in, gate_up, hidden_low)
    return (
        result,
        (
            inputs,
            scale_one,
            attn_in,
            queries,
            pair,
            log_sums,
            attended_low,
            middle,
            scale_two,
            ff_saved,
        ),
    )


def layer_backward(saved, grad_out, weights, info):
    qkv_full, out_full, gate_up_full, down_full, gains = weights
    (
        inputs,
        scale_one,
        attn_in,
        queries,
        pair,
        log_sums,
        attended_low,
        middle,
        scale_two,
        ff_saved,
    ) = saved
    cosine, sine = (info[0], info[1])
    rows, kv_local, groups, head_dim = queries.shape
    full_rows = pair.shape[1]
    ffn_in, gate_up, hidden_low = ff_saved
    grad_low = grad_out.astype(jnp.bfloat16)
    grad_down = jnp.einsum("rf,rd->fd", hidden_low, grad_low, preferred_element_type=jnp.float32)
    grad_hidden = jnp.einsum("rd,fd->rf", grad_low, down_full, preferred_element_type=jnp.float32)
    gate = gate_up[:, 0]
    sigma = jax.nn.sigmoid(gate)
    grad_gate = grad_hidden * gate_up[:, 1] * sigma * (1.0 + gate * (1.0 - sigma))
    grad_up = grad_hidden * gate * sigma
    grad_pair_ff = jnp.stack([grad_gate, grad_up], axis=1).astype(jnp.bfloat16)
    grad_gate_up = jnp.einsum(
        "rd,rtf->dtf", ffn_in, grad_pair_ff, preferred_element_type=jnp.float32
    )
    grad_ffn_in = lax.psum(
        jnp.einsum(
            "rtf,dtf->rd", grad_pair_ff, gate_up_full, preferred_element_type=jnp.float32
        ).astype(jnp.bfloat16),
        "tp",
    ).astype(jnp.float32)
    grad_mid_norm, grad_gain_two = plain_norm_back(middle, scale_two, gains[1], grad_ffn_in)
    grad_middle = grad_out + grad_mid_norm
    grad_attn_low = grad_middle.astype(jnp.bfloat16)
    grad_out_proj = jnp.einsum(
        "rh,rd->hd", attended_low, grad_attn_low, preferred_element_type=jnp.float32
    )
    grad_attended = jnp.einsum(
        "rd,hd->rh", grad_attn_low, out_full, preferred_element_type=jnp.float32
    ).astype(jnp.bfloat16)
    grad_queries, grad_pair = plain_attend_backward(
        queries, pair, log_sums, grad_attended.reshape(rows, kv_local, groups, head_dim), info
    )
    returned = lax.psum_scatter(
        grad_pair.reshape(2, full_rows, kv_local * head_dim).astype(jnp.bfloat16),
        "ctx",
        scatter_dimension=1,
        tiled=True,
    ).astype(jnp.float32)
    own_grad = returned.reshape(2, rows, kv_local, head_dim)
    grad_q_raw = rotate(grad_queries, cosine[:, None, None, :], -sine[:, None, None, :]).reshape(
        rows, kv_local, groups * head_dim
    )
    grad_k_raw = rotate(own_grad[0], cosine[:, None, :], -sine[:, None, :])
    grad_qkv = jnp.concatenate([grad_q_raw, grad_k_raw, own_grad[1]], axis=-1).astype(jnp.bfloat16)
    grad_qkv_proj = jnp.einsum("rd,rkc->dkc", attn_in, grad_qkv, preferred_element_type=jnp.float32)
    grad_attn_in = lax.psum(
        jnp.einsum("rkc,dkc->rd", grad_qkv, qkv_full, preferred_element_type=jnp.float32).astype(
            jnp.bfloat16
        ),
        "tp",
    ).astype(jnp.float32)
    grad_in_norm, grad_gain_one = plain_norm_back(inputs, scale_one, gains[0], grad_attn_in)
    grads = (
        grad_qkv_proj,
        grad_out_proj,
        grad_gate_up,
        grad_down,
        jnp.stack([grad_gain_one, grad_gain_two]),
    )
    return (grad_middle + grad_in_norm, grads)


def pick_section(is_first, first_value, second_value):
    return jnp.where(is_first, first_value, second_value)


def scale_by(factor, values):
    return values * factor


def local(boundary, segments, qkv_w, out_w, gate_up_w, down_w, norm_gains):
    micro_count = boundary.shape[1]
    rows = boundary.shape[3]
    width = boundary.shape[4]
    is_first = lax.axis_index("section") == 0
    ctx_index = lax.axis_index("ctx")
    local_ends = boundary[0, :, 0]
    seg_all = segments[:, 0]
    gathered = (
        lax.all_gather(qkv_w[0], ("fsdp", "ctx"), axis=0, tiled=True),
        lax.all_gather(out_w[0], ("fsdp", "ctx"), axis=1, tiled=True),
        lax.all_gather(gate_up_w[0], ("fsdp", "ctx"), axis=0, tiled=True),
        lax.all_gather(down_w[0], ("fsdp", "ctx"), axis=1, tiled=True),
        lax.all_gather(norm_gains[0], ("fsdp", "ctx"), axis=1, tiled=True),
    )
    weights = (gathered[0], gathered[1], gathered[2], gathered[3], gathered[4].astype(jnp.float32))
    chooser = partial(pick_section, is_first)
    received = jnp.zeros((rows, width), jnp.bfloat16)
    saved_list = []
    info_list = []
    outputs_list = []
    for tick_index in range(micro_count + 1):
        own_index = min(tick_index, micro_count - 1)
        prior_index = max(tick_index - 1, 0)
        seg_full = jnp.where(is_first, seg_all[own_index], seg_all[prior_index])
        info = context_info(seg_full, ctx_index, rows)
        inputs = jnp.where(is_first, local_ends[own_index], received).astype(jnp.float32)
        result, saved = layer_forward(inputs, weights, info)
        saved_list.append(saved)
        info_list.append(info)
        outputs_list.append(result)
        if tick_index < micro_count:
            received = from_behind(result.astype(jnp.bfloat16), "section", 1)
    grad_received = jnp.zeros((rows, width), jnp.float32)
    totals = None
    grad_list = []
    for tick_index in range(micro_count + 1):
        early = max(tick_index - 1, 0)
        late = min(tick_index + 1, micro_count)
        saved = jax.tree.map(chooser, saved_list[early], saved_list[late])
        info = jax.tree.map(chooser, info_list[early], info_list[late])
        own_grad = local_ends[min(tick_index, micro_count - 1)].astype(jnp.float32)
        grad_out = jnp.where(is_first, grad_received, own_grad)
        grad_inputs, grads = layer_backward(saved, grad_out, weights, info)
        valid = jnp.where(is_first, tick_index >= 1, tick_index < micro_count).astype(jnp.float32)
        grads = jax.tree.map(partial(scale_by, valid), grads)
        totals = grads if totals is None else jax.tree.map(jnp.add, totals, grads)
        grad_list.append(grad_inputs)
        if tick_index < micro_count:
            grad_received = from_behind(grad_inputs.astype(jnp.bfloat16), "section", -1).astype(
                grad_inputs.dtype
            )
    totals = (
        lax.psum_scatter(
            totals[0].astype(jnp.bfloat16), ("fsdp", "ctx"), scatter_dimension=0, tiled=True
        ).astype(jnp.float32),
        lax.psum_scatter(
            totals[1].astype(jnp.bfloat16), ("fsdp", "ctx"), scatter_dimension=1, tiled=True
        ).astype(jnp.float32),
        lax.psum_scatter(
            totals[2].astype(jnp.bfloat16), ("fsdp", "ctx"), scatter_dimension=0, tiled=True
        ).astype(jnp.float32),
        lax.psum_scatter(
            totals[3].astype(jnp.bfloat16), ("fsdp", "ctx"), scatter_dimension=1, tiled=True
        ).astype(jnp.float32),
        lax.psum_scatter(
            totals[4].astype(jnp.bfloat16), ("fsdp", "ctx"), scatter_dimension=1, tiled=True
        ).astype(jnp.float32),
    )
    ends_out = jnp.stack(
        [
            jnp.where(is_first, grad_list[micro_index + 1], outputs_list[micro_index + 1])
            for micro_index in range(micro_count)
        ]
    )
    return (
        ends_out[None, :, None],
        totals[0][None],
        totals[1][None],
        totals[2][None],
        totals[3][None],
        totals[4][0][None],
        totals[4][1][None],
    )


def swap_core(value):
    return lax.ppermute(value, "section", [(0, 1), (1, 0)])


def swap_tp(value):
    return lax.ppermute(value, "tp", [(0, 1), (1, 0)])


def swap_fsdp(value):
    return lax.ppermute(value, "fsdp", [(0, 1), (1, 0)])


def swap_ctx(value, m):
    return lax.ppermute(value, "ctx", [(i ^ m, i) for i in range(lax.axis_size("ctx"))])


def pick(bit, first, second):
    return jnp.where(bit == 0, first, second)


def ring(value):
    size = lax.axis_size("ctx")
    return lax.ppermute(value, "ctx", [(i, (i + 1) % size) for i in range(size)])


def ring_back(value):
    size = lax.axis_size("ctx")
    return lax.ppermute(value, "ctx", [((i + 1) % size, i) for i in range(size)])


class Flow:
    def __init__(self):
        self.values, self.next, self.last, self.first = {}, {}, None, None

    def put(self, name, n, value):
        self.values[name, n] = value

    def get(self, name, n):
        return self.values[name, n]

    def send(self, name, n, move, value, made=False):
        if self.last is not None:
            if made:
                self.next[self.last] = value
                self.first = value if self.first is None else self.first
            value, _ = lax.optimization_barrier((value, self.values[self.last]))
        self.put(name, n, move(value))
        self.last = (name, n)

    def point(self, name, n, value):
        names = DUE.get((name, n), ())
        if names or isinstance(value, tuple):
            ready = [self.next[k] for k in names if k in self.next]
            value, *got = lax.optimization_barrier((value, *[self.values[k] for k in names], *ready))
            self.values.update(zip(names, got))
        return value


def dot(a, b, dims):
    return lax.dot_general(a, b, (dims, ((), ())), preferred_element_type=f32)


NN = ((1,), (0,))
NT = ((1,), (1,))
TN = ((0,), (0,))
VMEM = pl.BlockSpec(memory_space=pltpu.VMEM)
SMEM = pl.BlockSpec(memory_space=pltpu.SMEM)
COST_SCALE = 0.1
VMEM_MIB = 28
A_MID, A_IN, ATT, S_MID, S_HALF, MIDDLE, B_MID, B_IN, HIDDEN, R_MID, R_HALF, RESULT = range(12)
G_MID, G_IN, D_HID, C_MID, C_HALF, D_MID, M_MID, M_IN, D_OUT, D_KEYS, D_QKV, E_MID, E_HALF, D_IN = range(12, 26)
A0, F0, F1, F2, F3, E0, E1, E2, E3, H1, H2, H3, HX, ATTN_SUM = range(14)
G1, G2, G3, GX, FFN_SUM, L1, L2, L3, LX, LOW_SUM, ENDS = range(17, 28)
DUE = {
    (HIDDEN, 0): ((ENDS, 1),),
    (RESULT, 0): ((F1, 1),),
    (S_MID, 1): ((F2, 1),),
    (C_MID, 1): ((G1, 1),),
    (M_MID, 1): ((L1, 1),),
    (D_OUT, 1): ((G2, 1),),
    (D_QKV, 1): ((L2, 1),),
    (D_IN, 1): ((G3, 1),),
    (D_HID, 0): ((L3, 1), (GX, 1)),
    (D_MID, 0): ((H3, 1), (LX, 1)),
    (D_OUT, 0): ((G1, 0),),
    (D_KEYS, 0): ((L1, 0), (HX, 1)),
    (D_IN, 0): ((H3, 0),),
}


def call(kernel, outs, ins, flops, name, **kw):
    args = dict(in_specs=[SMEM if v.dtype == jnp.int32 and v.ndim == 1 else VMEM for v in ins], out_specs=[VMEM] * len(outs))
    args.update(kw)
    return pl.pallas_call(
        kernel,
        out_shape=[jax.ShapeDtypeStruct(s, d) for s, d in outs],
        cost_estimate=pl.CostEstimate(flops=int(flops * COST_SCALE), bytes_accessed=1024, transcendentals=0),
        compiler_params=pltpu.CompilerParams(vmem_limit_bytes=VMEM_MIB * 2**20),
        name=name.__name__,
        **args,
    )(*ins)


def views(refs):
    return [r if k is None else r.at[k] for r in refs for k in ([None] if len(r.shape) == 2 else range(r.shape[0]))]


def block_spec(array, width, where):
    if array.ndim == 2:
        return pl.BlockSpec((array.shape[0], width), lambda t: (0, where(t)))
    return pl.BlockSpec(array.shape[:2] + (width,), lambda t: (0, 0, where(t)))


def cols(index, width):
    return pl.ds(pl.multiple_of(index * width, width), width)


def rope(x, cosine, sin_up, sin_down):
    return x * cosine + pltpu.roll(x, 96, 1) * sin_up + pltpu.roll(x, 32, 1) * sin_down


def kv_tables(cosine, sin_up, sin_down):
    is_key = lax.broadcasted_iota(jnp.int32, cosine.shape, 1) < HD
    return (jnp.where(is_key, cosine, 1.0), jnp.where(is_key, sin_up, 0.0), jnp.where(is_key, sin_down, 0.0))


def qkv_forward(order, spots, near, far, tables, blocks):
    rows, width = near.shape
    nb = order.shape[0]
    bw = width // nb
    qw = GROUPS * HD
    part_rows = rows // 4

    def kernel(order, spots, near, far, cosine, sin_up, sin_down, *refs):
        w, (q_ref, kv_ref, wide) = views(refs[:-3]), refs[-3:]
        for k in range(nb):
            wide[cols(order[k], bw), :] = w[k][:, : qw + 2 * HD]
        for part, a in enumerate((near, far)):
            for half in range(2):
                acc = dot(a[half * 2 * part_rows : (half + 1) * 2 * part_rows, :], wide[...], NN)
                for t in range(2):
                    there = cols(spots[4 * part + 2 * half + t], part_rows)
                    v = acc[t * part_rows : (t + 1) * part_rows, :]
                    tabs = (cosine[there, :], sin_up[there, :], sin_down[there, :])
                    for j in range(qw // 128):
                        here = slice(128 * j, 128 * (j + 1))
                        q_ref[there, here] = (rope(v[:, here], *tabs) * HD**-0.5).astype(bf16)
                    kv_ref[there, :] = rope(v[:, qw:], *kv_tables(*tabs)).astype(bf16)

    return call(
        kernel,
        [((2 * rows, qw), bf16), ((2 * rows, 2 * HD), bf16)],
        [order, spots, near, far, *tables, *blocks],
        2 * 2 * rows * width * (qw + 2 * HD),
        qkv_forward,
        scratch_shapes=[pltpu.VMEM((width, qw + 2 * HD), bf16)],
    )


def keep_mask(start, first, rows, keys):
    q_pos = first + lax.broadcasted_iota(jnp.int32, (rows, keys), 0)
    k_pos = lax.broadcasted_iota(jnp.int32, (rows, keys), 1)
    return jnp.where((k_pos <= q_pos) & (k_pos >= start), 0.0, masked_score)


def attend_forward(spots, q, kv, start):
    total, qw = q.shape
    rows = total // 4
    part_rows = total // 8

    def kernel(spots, q_ref, kv_ref, start_ref, att_ref, lse_ref):
        for i in range(4):
            here = slice(i * rows, (i + 1) * rows)
            keys = (i + 1) * rows
            k, v = kv_ref[:keys, :HD], kv_ref[:keys, HD:]
            bias = keep_mask(start_ref[here, :], i * rows, rows, keys)
            for g in range(GROUPS):
                head = slice(g * HD, (g + 1) * HD)
                s = dot(q_ref[here, head], k, NT) + bias
                top = jnp.max(s, axis=1, keepdims=True)
                p = jnp.exp(s - top)
                norm = jnp.sum(p, axis=1, keepdims=True)
                o = (dot(p.astype(bf16), v, NN) / norm).astype(bf16)
                for t in range(2):
                    att_ref[cols(spots[2 * i + t], part_rows), head] = o[t * part_rows : (t + 1) * part_rows, :]
                lse_ref[here, g : g + 1] = top + jnp.log(norm)

    return call(
        kernel,
        [((total, qw), bf16), ((total, GROUPS), f32)],
        [spots, q, kv, start],
        2 * 2 * total * total * qw,
        attend_forward,
    )


def attend_backward(spots, q, kv, lse, grad, start, tables):
    total, qw = q.shape
    rows = total // 4
    part_rows = total // 8

    def kernel(spots, q_ref, kv_ref, lse_ref, g_ref, start_ref, cosine, sin_up, sin_down, out, dq, dkv):
        dkv[...] = jnp.zeros_like(dkv)
        for i in range(4):
            here = slice(i * rows, (i + 1) * rows)
            keys = (i + 1) * rows
            k, v = kv_ref[:keys, :HD], kv_ref[:keys, HD:]
            bias = keep_mask(start_ref[here, :], i * rows, rows, keys)
            grads = jnp.concatenate([g_ref[cols(spots[2 * i + t], part_rows), :] for t in range(2)], axis=0)
            for g in range(GROUPS):
                head = slice(g * HD, (g + 1) * HD)
                qh, gh = q_ref[here, head], grads[:, head]
                p = jnp.exp(dot(qh, k, NT) + bias - lse_ref[here, g : g + 1])
                dp = dot(gh, v, NT)
                delta = jnp.sum(p * dp, axis=1, keepdims=True)
                ds = (p * (dp - delta)).astype(bf16)
                dq[here, head] = dot(ds, k, NN) * HD**-0.5
                dkv[:keys, :HD] += dot(ds, qh, TN)
                dkv[:keys, HD:] += dot(p.astype(bf16), gh, TN)
        for j in range(8):
            here, there = slice(j * part_rows, (j + 1) * part_rows), cols(spots[j], part_rows)
            tabs = (cosine[here, :], -sin_up[here, :], -sin_down[here, :])
            for b in range(qw // 128):
                out[there, 128 * b : 128 * (b + 1)] = rope(dq[here, 128 * b : 128 * (b + 1)], *tabs).astype(bf16)
            out[there, qw:] = rope(dkv[here, :], *kv_tables(*tabs)).astype(bf16)

    return call(
        kernel,
        [((total, qw + 2 * HD), bf16)],
        [spots, q, kv, lse, grad, start, *tables],
        5 * 2 * total * total * qw,
        attend_backward,
        scratch_shapes=[pltpu.VMEM((total, qw), f32), pltpu.VMEM((total, 2 * HD), f32)],
    )[0]


def project_out(order, values, blocks, first_col, out_type, part):
    total, depth = values.shape
    rows = total // 2
    nb = order.shape[0]
    bw = blocks[0].shape[-2]
    whole = first_col % depth != 0

    def kernel(order, v_ref, *refs):
        w, out = views(refs[:-1]), refs[-1]
        base = first_col if whole else 0
        for k in range(nb):
            acc = dot(v_ref[:, :bw], w[k][:, base : base + bw], NN)
            for j in range(1, depth // bw):
                acc += dot(v_ref[:, j * bw : (j + 1) * bw], w[k][:, base + j * bw : base + (j + 1) * bw], NN)
            out[:, cols(order[k], bw)] = acc.astype(out.dtype)

    return call(
        kernel,
        [((rows, nb * bw), out_type)],
        [order, values, *blocks],
        2 * rows * depth * nb * bw,
        project_out,
        grid=(1,),
        in_specs=[SMEM, pl.BlockSpec((rows, depth), lambda t: (part, 0))]
        + [block_spec(b, b.shape[-1] if whole else depth, lambda t: 0 if whole else first_col // depth) for b in blocks],
        out_specs=[pl.BlockSpec((rows, nb * bw), lambda t: (0, 0))],
    )[0]


def ffn_forward(order, near, far, blocks, units):
    rows, width = near.shape
    nb = order.shape[0]
    bw = width // nb
    tile = min(256, units)
    tiles = units // tile

    def kernel(order, near, far, *refs):
        hid, by_gate, by_up, wide = refs[-4:]
        w = views(refs[:-4])
        for k in range(nb):
            wide[0, cols(order[k], bw), :] = w[k][...]
            wide[1, cols(order[k], bw), :] = w[nb + k][...]
        for part, a in enumerate((near, far)):
            here = slice(part * rows, (part + 1) * rows)
            gate = dot(a[...], wide[0], NN)
            up = dot(a[...], wide[1], NN)
            sigma = 1.0 / (1.0 + jnp.exp(-gate))
            silu = gate * sigma
            hid[here, :] = (silu * up).astype(bf16)
            by_gate[here, :] = (up * sigma * (1.0 + gate * (1.0 - sigma))).astype(bf16)
            by_up[here, :] = silu.astype(bf16)

    all_rows = pl.BlockSpec((rows, width), lambda t: (0, 0))
    return call(
        kernel,
        [((2 * rows, units), bf16)] * 3,
        [order, near, far, *blocks, *blocks],
        2 * 2 * rows * width * 2 * units,
        ffn_forward,
        grid=(tiles,),
        in_specs=[SMEM, all_rows, all_rows]
        + [block_spec(b, tile, lambda t: t) for b in blocks]
        + [block_spec(b, tile, lambda t: t + tiles) for b in blocks],
        out_specs=[pl.BlockSpec((2 * rows, tile), lambda t: (0, t))] * 3,
        scratch_shapes=[pltpu.VMEM((2, width, tile), bf16)],
    )


def ffn_backward(order, near, far, by_gate, by_up, blocks):
    rows, width = near.shape
    nb = order.shape[0]
    units = by_gate.shape[1]
    bw = width // nb

    def kernel(order, near, far, by_gate, by_up, *refs):
        d_gate, d_up, wide = refs[-3:]
        w = views(refs[:-3])
        for k in range(nb):
            wide[:, cols(order[k], bw)] = w[k][...]
        for part, a in enumerate((near, far)):
            here = slice(part * rows, (part + 1) * rows)
            acc = dot(a[...], wide[...], NT)
            d_gate[here, :] = (acc * by_gate[here, :].astype(f32)).astype(bf16)
            d_up[here, :] = (acc * by_up[here, :].astype(f32)).astype(bf16)

    all_rows = pl.BlockSpec((rows, width), lambda t: (0, 0))
    tall = pl.BlockSpec((2 * rows, bw), lambda t: (0, t))
    return call(
        kernel,
        [((2 * rows, units), bf16)] * 2,
        [order, near, far, by_gate, by_up, *blocks],
        2 * 2 * rows * width * units,
        ffn_backward,
        grid=(units // bw,),
        in_specs=[SMEM, all_rows, all_rows, tall, tall]
        + [block_spec(b, bw, lambda t: 2 * units // bw + t) for b in blocks],
        out_specs=[tall] * 2,
        scratch_shapes=[pltpu.VMEM((bw, width), bf16)],
    )


def ffn_input_grad(order, d_gate, d_up, blocks):
    total, units = d_gate.shape
    rows = total // 2
    nb = order.shape[0]
    bw = blocks[0].shape[-2]

    def kernel(order, dg, du, *refs):
        far, near, slots, sems = refs[-4:]
        w = views(refs[:-4])

        def fetch(k):
            return pltpu.make_async_copy(w[k].at[:, : 2 * units], slots.at[k % 2], sems.at[k % 2])

        fetch(0).start()
        for k in range(nb):
            if k + 1 < nb:
                fetch(k + 1).start()
            fetch(k).wait()
            here = cols(order[k], bw)
            for out, part in ((near, 0), (far, 1)):
                tokens = slice(part * rows, (part + 1) * rows)
                acc = dot(dg[tokens, :], slots[k % 2, :, :units], NT) + dot(du[tokens, :], slots[k % 2, :, units:], NT)
                out[:, here] = acc.astype(out.dtype)

    return call(
        kernel,
        [((rows, nb * bw), bf16), ((rows, nb * bw), f32)],
        [order, d_gate, d_up, *blocks],
        2 * total * 2 * units * nb * bw,
        ffn_input_grad,
        in_specs=[SMEM, VMEM, VMEM] + [pl.BlockSpec(memory_space=pl.ANY)] * len(blocks),
        scratch_shapes=[pltpu.VMEM((2, bw, 2 * units), bf16), pltpu.SemaphoreType.DMA((2,))],
    )


def block_columns(rows, width, places):
    return [pl.BlockSpec((rows, width), lambda t, order, p=p: (0, order[p])) for p in places for _ in range(4)]


def turn(left, first, turned):
    rows, width = left[0].shape
    for p in range(len(left) // 4):
        for part in range(2):
            turned[p * width : (p + 1) * width, part * rows : (part + 1) * rows] = left[4 * p + first + part][...].T


def store(out, acc, got, here=slice(None)):
    width = out.shape[1]
    for p in range(out.shape[0]):
        value = acc[p * width : (p + 1) * width]
        for r in got:
            value += r[p, :, here].astype(f32)
        out[p, :, here] = value.astype(bf16)


def ffn_grad(order, near, far, d_gate, d_up, hidden, grad_near, grad_far, side, m, *received):
    total, units = d_gate.shape
    rows, width = near.shape
    bw = width // order.shape[0]
    tile = min(512, units // 2)
    tiles = units // tile
    steps = tiles if side else 2 * tiles
    begin = 2 * tiles * side

    def kernel(order, dg, du, h, *refs):
        left, got, out, turned = refs[:8], refs[8:-2], refs[-2], refs[-1]
        step = pl.program_id(0)
        t = step + begin
        pl.when((step == 0) & (t < 2 * tiles))(lambda: turn(left, 0, turned))
        pl.when(t == 2 * tiles)(lambda: turn(left, 2, turned))
        pl.when(t < tiles)(lambda: store(out, dot(turned[...], dg[...], NN), got))
        pl.when((t >= tiles) & (t < 2 * tiles))(lambda: store(out, dot(turned[...], du[...], NN), got))
        pl.when(t >= 2 * tiles)(lambda: store(out, dot(turned[...], h[...], NN), got))

    def tall(first):
        return pl.BlockSpec((total, tile), lambda t, order: (0, jnp.clip(t + begin - first * tiles, 0, tiles - 1)))

    part = pl.BlockSpec((2, bw, tile), lambda t, order: (0, 0, t))
    return pl.pallas_call(
        kernel,
        out_shape=jax.ShapeDtypeStruct((2, bw, steps * tile), bf16),
        grid_spec=pltpu.PrefetchScalarGridSpec(
            num_scalar_prefetch=1,
            grid=(steps,),
            in_specs=[tall(0), tall(1), tall(2)] + block_columns(rows, bw, (2 * m, 2 * m + 1)) + [part] * len(received),
            out_specs=part,
            scratch_shapes=[pltpu.VMEM((2 * bw, total), bf16)],
        ),
        cost_estimate=pl.CostEstimate(flops=int(4 * total * steps * tile * bw * COST_SCALE), bytes_accessed=1024, transcendentals=0),
        compiler_params=pltpu.CompilerParams(vmem_limit_bytes=VMEM_MIB * 2**20),
        name=ffn_grad.__name__,
    )(order, d_gate, d_up, hidden, *([near, far, grad_near, grad_far] * 2), *received)


def attn_grad(order, near, far, d_qkv, attended, grad_near, grad_far, m, *received):
    total, nq = d_qkv.shape
    rows, width = near.shape
    bw = width // order.shape[0]

    def kernel(order, dq, att, *refs):
        left, got, out = refs[:8], refs[8:-1], refs[-1]
        for p in range(2):
            near, far, gn, gf = left[4 * p : 4 * p + 4]
            value = dot(near[...], dq[:rows, :], TN) + dot(far[...], dq[rows:, :], TN)
            for r in got:
                value += r[p, :, :nq].astype(f32)
            out[p, :, :nq] = value.astype(bf16)
            value = dot(att[:rows, :], gn[...], TN) + dot(att[rows:, :], gf[...], TN)
            for r in got:
                value += r[p, :, nq:].astype(f32)
            out[p, :, nq:] = value.astype(bf16)

    def whole(shape):
        return pl.BlockSpec(shape, lambda t, order: (0,) * len(shape))

    shape = (2, bw, nq + bw)
    return pl.pallas_call(
        kernel,
        out_shape=jax.ShapeDtypeStruct(shape, bf16),
        grid_spec=pltpu.PrefetchScalarGridSpec(
            num_scalar_prefetch=1,
            grid=(1,),
            in_specs=[whole(d_qkv.shape), whole(attended.shape)]
            + block_columns(rows, bw, (2 * m, 2 * m + 1))
            + [whole(shape)] * len(received),
            out_specs=whole(shape),
        ),
        cost_estimate=pl.CostEstimate(flops=int(4 * total * (nq + bw) * bw * COST_SCALE), bytes_accessed=1024, transcendentals=0),
        compiler_params=pltpu.CompilerParams(vmem_limit_bytes=VMEM_MIB * 2**20),
        name=attn_grad.__name__,
    )(order, d_qkv, attended, *([near, far, grad_near, grad_far] * 2), *received)


def out_backward(order, near, far, blocks):
    rows, width = near.shape
    nb = order.shape[0]
    bw = width // nb
    qw = GROUPS * HD

    def kernel(order, near, far, *refs):
        w, out = views(refs[:-1]), refs[-1]
        for part, a in enumerate((near, far)):
            acc = dot(a[:, cols(order[0], bw)], w[0][:, qw + 2 * HD :], NT)
            for k in range(1, nb):
                acc += dot(a[:, cols(order[k], bw)], w[k][:, qw + 2 * HD :], NT)
            out[part * rows : (part + 1) * rows, :] = acc.astype(bf16)

    return call(
        kernel, [((2 * rows, qw), bf16)], [order, near, far, *blocks], 2 * 2 * rows * width * qw, out_backward
    )[0]


def qkv_backward(order, d_qkv, blocks):
    total, nq = d_qkv.shape
    rows = total // 2
    nb = order.shape[0]
    bw = blocks[0].shape[-2]

    def kernel(order, d_ref, *refs):
        w, (far_out, near_out) = views(refs[:-2]), refs[-2:]
        for k in range(nb):
            here = cols(order[k], bw)
            far_out[:, here] = dot(d_ref[rows:, :], w[k][:, :nq], NT).astype(bf16)
            near_out[:, here] = dot(d_ref[:rows, :], w[k][:, :nq], NT)

    return call(
        kernel,
        [((rows, nb * bw), bf16), ((rows, nb * bw), f32)],
        [order, d_qkv, *blocks],
        2 * total * nb * bw * nq,
        qkv_backward,
    )


def gather_group(flow, point, n, block):
    half = block.shape[0] // 2
    beside, pair, far_block = flow.point(point, n, (swap_tp(block), swap_fsdp(block), swap_core(block)))
    last = jnp.concatenate((swap_tp(pair[:half]), swap_fsdp(beside[half:])), axis=0)
    far_pair, far_beside = swap_core(pair), swap_core(beside)
    last, far_pair, far_beside = flow.point(point + 1, n, (last, far_pair, far_beside))
    near = jnp.concatenate((block, beside, pair, last), axis=0)
    return (near, jnp.concatenate((far_block, far_beside, far_pair, swap_core(last)), axis=0))


def sum_group(flow, point, n, near, far):
    half = far.shape[0] // 2
    high = flow.point(point, n, near[half:] + swap_core(far[half:]).astype(f32))
    low = near[:half] + swap_core(far[:half]).astype(f32)
    half //= 2
    split = half // 2
    last = high[half:].astype(bf16)
    by_tp, by_fsdp = flow.point(point + 1, n, (swap_tp(last[:split]), swap_fsdp(last[split:])))
    pair = jnp.concatenate((high[:split] + by_tp.astype(f32), high[split:half]), axis=0).astype(bf16)
    beside = jnp.concatenate((low[half : half + split], low[half + split :] + by_fsdp.astype(f32)), axis=0).astype(bf16)
    return low[:half] + swap_tp(beside).astype(f32) + swap_fsdp(pair).astype(f32)


def row_scale(values):
    return lax.rsqrt(jnp.mean(values * values, axis=-1, keepdims=True) + norm_eps)


def group_layer(flow, n, state, attn_w, gains, order, spots, start, tables):
    scale_one = row_scale(state)
    a_near, a_far = gather_group(flow, A_MID, n, (state * scale_one * gains[0]).astype(bf16))
    q, kv = qkv_forward(order, spots, a_near, a_far, tables, attn_w)
    attended, lse = attend_forward(spots, q, kv, start)
    attended = flow.point(ATT, n, attended)
    first_col = kv.shape[1] + q.shape[1]
    far = project_out(order, attended, attn_w, first_col, bf16, 1)
    near = project_out(order, attended, attn_w, first_col, f32, 0)
    middle = flow.point(MIDDLE, n, state + sum_group(flow, S_MID, n, near, far))
    scale_two = row_scale(middle)
    b_near, b_far = gather_group(flow, B_MID, n, (middle * scale_two * gains[1]).astype(bf16))
    ffn_w = [flow.get(k, n) for k in ((F0, F1, F2, F3) if n else (F0, E0, F1, E1, F2, E2, F3, E3))]
    units = ffn_w[0].shape[-1] // 3
    hidden, by_gate, by_up = ffn_forward(order, b_near, b_far, ffn_w, units)
    hidden = flow.point(HIDDEN, n, hidden)
    far = project_out(order, hidden, ffn_w, 2 * units, bf16, 1)
    near = project_out(order, hidden, ffn_w, 2 * units, f32, 0)
    result = flow.point(RESULT, n, middle + sum_group(flow, R_MID, n, near, far))
    kept = (attn_w, ffn_w, state, scale_one, a_near, a_far, q, kv, attended, lse)
    return (result, kept + (middle, scale_two, b_near, b_far, hidden, by_gate, by_up))


def norm_back(values, scale_rows, gain, grad_normed):
    scaled = values * scale_rows
    grad_gain = jnp.sum(grad_normed * scaled, axis=0)
    grad_hat = grad_normed * gain
    grad_in = scale_rows * (grad_hat - scaled * jnp.mean(grad_hat * scaled, axis=-1, keepdims=True))
    return (grad_in, grad_gain)


def send_back(flow, n, makes, names):
    last = [make(3) for make in makes]
    for m in (2, 1, 0):
        for k, make in enumerate(makes):
            flow.send(names[k][2 - m], n, ring_back, last[k], True)
        last = [make(m, flow.get(names[k][2 - m], n)) for k, make in enumerate(makes)]
        if m:
            yield last[0]
    for k in range(len(makes)):
        flow.put(names[k][3], n, swap_fsdp(last[k][1]))
        flow.put(names[k][4], n, last[k][0])
    yield last[0]


def group_layer_back(flow, n, saved, grad_out, gains, order, spots, start, tables):
    (attn_w, ffn_w, state, scale_one, a_near, a_far, q, kv, attended, lse) = saved[:10]
    (middle, scale_two, b_near, b_far, hidden, by_gate, by_up) = saved[10:]
    g_near, g_far = gather_group(flow, G_MID, n, grad_out.astype(bf16))
    d_gate, d_up = ffn_backward(order, g_near, g_far, by_gate, by_up, ffn_w)
    d_gate = flow.point(D_HID, n, d_gate)
    makes = [partial(ffn_grad, order, b_near, b_far, d_gate, d_up, hidden, g_near, g_far, side) for side in range(2)]
    rounds = send_back(flow, n, makes, ((G1, G2, G3, GX, FFN_SUM), (L1, L2, L3, LX, LOW_SUM)))
    next(rounds)
    if n:
        next(rounds), next(rounds)
        d_gate, _ = lax.optimization_barrier((d_gate, flow.first))
    far, near = ffn_input_grad(order, d_gate, d_up, ffn_w)
    grad_mid, gain_two = norm_back(middle, scale_two, gains[1], sum_group(flow, C_MID, n, near, far))
    grad_mid = flow.point(D_MID, n, grad_mid + grad_out)
    m_near, m_far = gather_group(flow, M_MID, n, grad_mid.astype(bf16))
    d_att = flow.point(D_OUT, n, out_backward(order, m_near, m_far, attn_w))
    d_qkv = flow.point(D_KEYS, n, attend_backward(spots, q, kv, lse, d_att, start, tables))
    far, near = qkv_backward(order, d_qkv, attn_w)
    make_attn = partial(attn_grad, order, a_near, a_far, d_qkv, attended, m_near, m_far)
    for _ in send_back(flow, n, [make_attn], ((H1, H2, H3, HX, ATTN_SUM),)):
        pass
    for _ in rounds:
        pass
    far = flow.point(D_QKV, n, far)
    grad_in, gain_one = norm_back(state, scale_one, gains[0], sum_group(flow, E_MID, n, near, far))
    return (flow.point(D_IN, n, grad_mid + grad_in), (gain_one, gain_two))


def local_group(boundary, segments, qkv_w, out_w, gate_up_w, down_w, norm_gains):
    nz = lax.axis_size("ctx")
    s, x, z, y = (lax.axis_index(a) for a in ("section", "fsdp", "ctx", "tp"))
    rows, width = boundary.shape[3:]
    own_rows = rows // 2

    ends = lax.dynamic_slice_in_dim(boundary[0, :, 0], y * own_rows, own_rows, axis=1)

    def moves(micro, core):
        return [
            ((core * 2 + f) * nz + c, (c // 2 * 2 + c % 2) * nz + 2 * micro + f) for f in range(2) for c in range(nz)
        ]

    axes = ("section", "fsdp", "ctx")
    late = lax.div(z, 2)
    came = [lax.ppermute(ends[t], axes, moves(t, 0)) for t in range(2)]
    state = pick(late, came[0], came[1]).astype(f32)

    g = norm_gains[0].astype(f32)
    other = swap_core(g)
    g = jnp.concatenate([pick(s, g, other), pick(s, other, g)], axis=0)
    bit = 1
    while bit < nz:
        other = swap_ctx(g, bit)
        side = lax.rem(lax.div(z, bit), 2)
        g = jnp.concatenate([pick(side, g, other), pick(side, other, g)], axis=1)
        bit *= 2
    other = swap_fsdp(g)
    gains = jnp.concatenate([pick(x, g, other), pick(x, other, g)], axis=1).reshape(2, 2, width)

    def parts_of(cut):
        mine, pair = cut(x, s), cut(1 - x, s)
        got = swap_core(jnp.stack([cut(x, 1 - s), cut(1 - x, 1 - s)]))
        return [(pick(s ^ k, mine, got[0]), pick(s ^ k, pair, got[1])) for k in range(2)]

    heads = qkv_w.shape[3]
    head_rows = out_w.shape[1] // 4
    units = gate_up_w.shape[3] // 4
    block = qkv_w.shape[1]
    qkv_own = qkv_w[0].reshape(block, -1)

    def cut_attn(p, c):
        k = 2 * p + c
        left = lax.dynamic_slice_in_dim(qkv_own, k * heads, heads, axis=1)
        right = lax.dynamic_slice_in_dim(out_w[0], k * head_rows, head_rows, axis=0)
        return jnp.concatenate([left, right], axis=1)

    def cut_ffn(p, c):
        k = 2 * p + c
        gate_up = lax.dynamic_slice_in_dim(gate_up_w[0], k * units, units, axis=2)
        down = lax.dynamic_slice_in_dim(down_w[0], k * units, units, axis=0)
        panels = [down[j * block : (j + 1) * block] for j in range(units // block)]
        return jnp.concatenate([gate_up[:, 0], gate_up[:, 1]] + panels, axis=1)

    flow = Flow()

    attn_parts = parts_of(cut_attn)
    pairs = swap_fsdp(jnp.stack([attn_parts[n][1] for n in range(2)]))
    line = [jnp.stack([attn_parts[0][0], pairs[0], attn_parts[1][0], pairs[1]])]
    line[0], state = lax.optimization_barrier((line[0], state))
    gate_up_w, down_w, first, gains = lax.optimization_barrier((gate_up_w, down_w, line[0], gains))
    line = [first]
    for m in range(3):
        flow.send(A0, m, ring, line[-1])
        line.append(flow.get(A0, m))
    attn_w = [[v[2 * n : 2 * n + 2] for v in line] for n in range(2)]
    ffn_parts = parts_of(cut_ffn)
    flow.put(F0, 0, ffn_parts[0][0])
    flow.put(E0, 0, swap_fsdp(ffn_parts[0][1]))
    for m in range(3):
        flow.send((F1, F2, F3)[m], 0, ring, flow.get((F0, F1, F2)[m], 0))
        flow.send((E1, E2, E3)[m], 0, ring, flow.get((E0, E1, E2)[m], 0))
    flow.put(F0, 1, jnp.stack([ffn_parts[1][0], swap_fsdp(ffn_parts[1][1])]))
    for m in range(3):
        flow.send((F1, F2, F3)[m], 1, ring, flow.get((F0, F1, F2)[m], 1))
    ends, _ = lax.optimization_barrier((ends, flow.get(E3, 0)))
    came = [lax.ppermute(ends[t], axes, moves(t, 1)) for t in range(2)]
    flow.put(ENDS, 1, pick(late, came[0], came[1]))

    order = jnp.stack([(x ^ i) * nz + lax.rem(z + nz - m, nz) for m in range(nz) for i in range(2)]).astype(jnp.int32)

    spots = jnp.stack([(4 * s + 2 * x + y) ^ k for k in range(8)]).astype(jnp.int32)
    batch = lax.rem(z, 2)
    seg_here = segments[:, 0].astype(f32)
    seg_all = pick(batch ^ x, seg_here, swap_fsdp(seg_here))
    seg = pick(late, seg_all[0], seg_all[1])
    start = jnp.sum((seg[None, :] < seg[:, None]).astype(jnp.int32), axis=1)
    pos = jnp.arange(seg.shape[0], dtype=jnp.int32)
    lane = jnp.arange(128)
    inverse = rope_base ** (-2.0 * (lane % (HD // 2)).astype(f32) / HD)
    angles = (pos - start).astype(f32)[:, None] * inverse[None, :]
    cosine, sine = jnp.cos(angles), jnp.sin(angles)
    low_half = (lane % HD) < HD // 2
    tables = (cosine, jnp.where(low_half, -sine, 0.0), jnp.where(low_half, 0.0, sine))

    start = start[:, None]
    state, kept_0 = group_layer(flow, 0, state, attn_w[0], gains[0], order, spots, start, tables)
    state = state.astype(bf16).astype(f32)
    final, kept_1 = group_layer(flow, 1, state, attn_w[1], gains[1], order, spots, start, tables)

    grad, gains_1 = group_layer_back(flow, 1, kept_1, flow.get(ENDS, 1).astype(f32), gains[1], order, spots, start, tables)
    grad, gains_0 = group_layer_back(flow, 0, kept_0, grad, gains[0], order, spots, start, tables)
    grads = [
        [(flow.get(own, n), flow.get(pair, n)) for own, pair in ((ATTN_SUM, HX), (FFN_SUM, GX), (LOW_SUM, LX))]
        for n in range(2)
    ]
    gain_grads = [gains_0, gains_1]

    g = [jnp.stack(pair) for pair in gain_grads]
    g = pick(s, g[0], g[1]) + swap_core(pick(s, g[1], g[0]))

    def fold(value, side, swap):
        half = value.shape[1] // 2
        first, second = value[:, :half], value[:, half:]
        return pick(side, first, second) + swap(pick(side, second, first))

    g = fold(g, x, swap_fsdp)
    g = g + swap_tp(g)
    g, _ = lax.optimization_barrier((g, flow.get(L3, 0)))
    bit = nz // 2
    while bit:
        g = fold(g, lax.rem(lax.div(z, bit), 2), lambda v: swap_ctx(v, bit))
        bit //= 2

    grad, final, g = lax.optimization_barrier((grad, final, g))
    went = [
        [lax.ppermute(v.astype(bf16), axes, [(b, a) for a, b in moves(t, core)]) for t in range(2)]
        for core, v in enumerate((grad, final))
    ]
    both = jnp.stack([pick(s, went[0][t], went[1][t]) for t in range(2)])
    other = swap_tp(both)
    ends_out = jnp.concatenate([pick(y, both, other), pick(y, other, both)], axis=1).astype(f32)

    def settle(which):
        (mine_0, pair_0), (mine_1, pair_1) = grads[0][which], grads[1][which]
        mine, pair = pick(s, mine_0, mine_1), pick(s, pair_0, pair_1)
        got = swap_core(jnp.stack([pick(s, mine_1, mine_0), pick(s, pair_1, pair_0)]))
        first = (pick(x, mine, pair), pick(x, got[0], got[1]))
        second = (pick(x, pair, mine), pick(x, got[1], got[0]))
        return [pick(s ^ c, *half) for half in (first, second) for c in range(2)]

    attn = settle(0)
    grad_qkv = jnp.stack([v[:, :heads] for v in attn], axis=1).astype(f32)
    grad_out = jnp.concatenate([v[:, heads:] for v in attn], axis=0).astype(f32)
    ffn = settle(1)
    grad_gate_up = jnp.stack(
        [jnp.concatenate([v[:, t * units : (t + 1) * units] for v in ffn], axis=1) for t in range(2)], axis=1
    ).astype(f32)
    grad_down = jnp.concatenate(settle(2), axis=1).T.astype(f32)

    return (ends_out[None, :, None], grad_qkv[None], grad_out[None], grad_gate_up[None], grad_down[None], g[0][None], g[1][None])


def solution(mesh):
    size = mesh.shape
    grouped = size["section"] == size["fsdp"] == size["tp"] == 2 and size["ctx"] == 4 and KV // size["tp"] == 4
    return jax.shard_map(
        local_group if grouped else local,
        mesh=mesh,
        in_specs=(
            P("section", None, "fsdp", "ctx", None),
            P(None, "fsdp", None),
            P("section", ("fsdp", "ctx"), "tp", None),
            P("section", "tp", ("fsdp", "ctx")),
            P("section", ("fsdp", "ctx"), None, "tp"),
            P("section", "tp", ("fsdp", "ctx")),
            P("section", None, ("fsdp", "ctx")),
        ),
        out_specs=(
            P("section", None, "fsdp", "ctx", None),
            P("section", ("fsdp", "ctx"), "tp", None),
            P("section", "tp", ("fsdp", "ctx")),
            P("section", ("fsdp", "ctx"), None, "tp"),
            P("section", "tp", ("fsdp", "ctx")),
            P("section", ("fsdp", "ctx")),
            P("section", ("fsdp", "ctx")),
        ),
        check_vma=False,
    )
```
